32 devices in a mesh: blk: 2 (over x), mblk: 16 (over z, y, core).
Axes of the slice: x: 2, y: 2, z: 4, core: 2. Of those that a mesh axis runs over, the one named last changes fastest.
Arguments:
- pixels: float32 [512, 1024], P(('blk', 'mblk')), may hold values from -6 to 6
- block_ids: int32 [512], P(('blk', 'mblk')), may hold values from 0 to 511, as said below
- block_mask: int32 [512], P(('blk', 'mblk')), may hold values 0 or 1
- model_cl: float32 [4096], replicated, may hold values from 0.5 to 1.5
Outputs:
- pseudo_cl: float32 [4096], replicated
- misfit: float32 [], replicated
The draws below stay inside these ranges and needn't reach their ends.
Inputs may be any that keep to these rules, and one draw needn't show every extreme that they name: block_ids holds every block number once. The device at blk index s and mblk index j holds, for every blk index b, exactly 8 blocks of the cycles of the device at blk index b and mblk index j, where cycle r belongs to the device at blk index r // 32 and mblk index (r % 32) // 2.
All inputs are finite; a program needn't handle non-finite values. No bound on the sum of `block_mask` on one device may be relied on, other than what follows from the above.
Results may differ from the reference program's by a relative error of at most 0.0003.
Values sent between devices are 32-bit elements; how exact they have to be, the bound alone decides.
No kernel may reach another device: no remote copies, remote signals or barrier semaphores. Data moves between devices by JAX's collectives and lax.ppermute only.
A program may use at most 64 MiB of HBM per device.

```python
import math
import jax
import jax.numpy as jnp
from jax import lax

NSIDE = 2048
CYCLE_PIX = 8192
LMAX = 4096
BLOCK_PIX = 1024
CYCLES = 64
SLOTS = 16
CAP = 8
BLOCKS = 512
N_BLK = 2
N_MBLK = 16


def draw_block_ids(key, part):
    owner_key, slot_key = jax.random.split(key)
    owner_total = N_BLK * N_MBLK
    owner_perm = jax.vmap(lambda sub_key: jax.random.permutation(sub_key, SLOTS))(jax.random.split(owner_key, owner_total))
    slot_perm = jax.vmap(lambda sub_key: jax.random.permutation(sub_key, SLOTS))(jax.random.split(slot_key, owner_total))
    source = jnp.arange(N_BLK, dtype=jnp.int32)[:, None, None]
    column = jnp.arange(N_MBLK, dtype=jnp.int32)[None, :, None]
    initial = slot_perm.reshape(N_BLK, N_MBLK, SLOTS).astype(jnp.int32)
    band_idx = initial // CAP
    within = initial % CAP
    owner = band_idx * N_MBLK + column
    picked = owner_perm.astype(jnp.int32)[owner, source * CAP + within]
    return (owner * SLOTS + picked).reshape(-1).astype(jnp.int32)


def plant(entries, key, smallest, top_value):
    shape = entries.shape
    place = [jax.random.randint(jax.random.fold_in(key, axis), (), 0, shape[axis]) for axis in range(len(shape))]
    entries = entries.at[tuple(place)].set(smallest)
    longest = shape.index(max(shape))
    place[longest] = (place[longest] + 1) % shape[longest]
    return entries.at[tuple(place)].set(top_value)


def levels(key, dims, pieces, low, largest):
    def one(position, parts):
        steps = jax.random.uniform(jax.random.fold_in(jax.random.fold_in(key, 6), position), (parts,), jnp.float32, low / len(pieces), largest / len(pieces))
        return jnp.repeat(jnp.exp(steps), dims[position] // parts).reshape((-1,) + (1,) * (len(dims) - position - 1))

    loudness = one(*pieces[0])
    for cut in pieces[1:]:
        loudness = loudness * one(*cut)
    return loudness


def scatter_about(rng, shape, scale, limit, cuts=(), kind=jnp.bfloat16):
    array = scale * jax.random.normal(rng, shape, jnp.float32)
    if cuts:
        array = array * levels(rng, shape, cuts, -0.22, 0.18)
    return jnp.clip(array, -limit, limit).astype(kind)


def setup_inputs(seed: int = 0) -> dict:
    keys = jax.random.split(jax.random.key(seed), 5)
    pixels = scatter_about(keys[0], (BLOCKS, BLOCK_PIX), 1.0, 6.0, ((0, 32),), jnp.float32)
    block_ids = draw_block_ids(jax.random.fold_in(keys[4], 71), 0)
    block_mask = plant((jax.random.randint(keys[2], (BLOCKS,), 0, 4) < 3).astype(jnp.int32), jax.random.fold_in(keys[2], 1), 0, 1)
    model_cl = jnp.clip(jax.random.uniform(keys[3], (LMAX,), jnp.float32, 0.5, 1.5), 0.5, 1.5)
    return {"pixels": pixels, "block_ids": block_ids, "block_mask": block_mask, "model_cl": model_cl}


def log_products(degree_count):
    counter = jnp.arange(1, degree_count, dtype=jnp.int32).astype(jnp.float32)
    return jnp.concatenate([jnp.zeros((1,), jnp.float32), jnp.cumsum(jnp.log1p(-0.5 / counter))])

def seeds_for(latitude, orders_f, log_prod):
    base_log = 0.5 * (jnp.log(2.0 * orders_f + 1.0) - math.log(4.0 * math.pi)) + 0.5 * log_prod
    return jnp.exp(base_log[None, :] + 0.5 * orders_f[None, :] * jnp.log1p(-latitude[:, None] * latitude[:, None]))

def coefficients(degree_f, orders_f):
    alpha_term = jnp.sqrt((2.0 * degree_f - 1.0) * (2.0 * degree_f + 1.0) / jnp.maximum((degree_f - orders_f) * (degree_f + orders_f), 1.0))
    beta_term = alpha_term * jnp.sqrt(jnp.maximum((degree_f - 1.0 - orders_f) * (degree_f - 1.0 + orders_f), 0.0) / jnp.maximum((2.0 * degree_f - 3.0) * (2.0 * degree_f - 1.0), 1.0))
    return (alpha_term, beta_term)

def advance(degree, orders, latitude, prev_one, prev_two, seed_vals):
    degree_f = degree.astype(jnp.float32)
    orders_f = orders.astype(jnp.float32)
    alpha_term, beta_term = coefficients(degree_f, orders_f)
    grown = alpha_term[None, :] * latitude[:, None] * prev_one - beta_term[None, :] * prev_two
    return jnp.where(degree > orders[None, :], grown, jnp.where(degree == orders[None, :], seed_vals, 0.0))

def reference(pixels, block_ids, block_mask, model_cl):
    kept = pixels * block_mask[:, None].astype(jnp.float32)
    cycle_map = jnp.zeros_like(kept).at[block_ids].set(kept).reshape(CYCLES, CYCLE_PIX)
    cycle_idx = jnp.arange(CYCLES, dtype=jnp.int32)
    latitude = (CYCLES // 2 - cycle_idx).astype(jnp.float32) * (2.0 / (3.0 * NSIDE))
    half_shift = jnp.where(cycle_idx % 2 == 0, 0.5, 0.0).astype(jnp.float32)
    full_fft = jnp.fft.rfft(cycle_map, axis=1)[:, :LMAX]
    raw_re = jnp.real(full_fft)
    raw_im = jnp.imag(full_fft)
    orders = jnp.arange(LMAX, dtype=jnp.int32)
    orders_f = orders.astype(jnp.float32)
    phase_angle = half_shift[:, None] * orders_f[None, :] * (2.0 * math.pi / CYCLE_PIX)
    phase_cos = jnp.cos(phase_angle)
    phase_sin = jnp.sin(phase_angle)
    spec_re = raw_re * phase_cos + raw_im * phase_sin
    spec_im = raw_im * phase_cos - raw_re * phase_sin
    seed_vals = seeds_for(latitude, orders_f, log_products(LMAX))
    norm_scale = math.sqrt(4.0 * math.pi / (CYCLES * CYCLE_PIX))

    def advance_row(carried, degree):
        prev_one, prev_two = carried
        fresh_row = advance(degree, orders, latitude, prev_one, prev_two, seed_vals)
        row_re = lax.optimization_barrier(jnp.sum(fresh_row * spec_re, axis=0)) * norm_scale
        row_im = lax.optimization_barrier(jnp.sum(fresh_row * spec_im, axis=0)) * norm_scale
        return ((fresh_row, prev_one), (row_re, row_im))
    zero_state = jnp.zeros((CYCLES, LMAX), jnp.float32)
    _, (alm_re, alm_im) = lax.scan(advance_row, (zero_state, zero_state), orders)
    weights = jnp.where(orders == 0, 1.0, 2.0).astype(jnp.float32)
    power_sum = lax.optimization_barrier(jnp.sum(weights[None, :] * (alm_re * alm_re + alm_im * alm_im), axis=1))
    pseudo_cl = power_sum / (2.0 * orders_f + 1.0)
    rel_error = (pseudo_cl - model_cl) / model_cl
    misfit = jnp.mean(rel_error * rel_error)
    return (pseudo_cl, misfit)
```

```python
import functools
import math

import jax
import jax.numpy as jnp
import numpy as np
from jax import lax
from jax.experimental import pallas as pl
from jax.experimental.pallas import tpu as pltpu
from jax.sharding import PartitionSpec as P

NSIDE = 2048
CYCLE_PIX = 8192
LMAX = 4096
BLOCK_PIX = 1024
SEGS = 8
LANES = 128
HIGHEST = lax.Precision.HIGHEST


def dft_tables(n_dev):
    width = CYCLE_PIX // n_dev
    pairs = LMAX // (2 * n_dev)
    a = np.arange(n_dev)
    p2 = np.arange(n_dev)
    p1 = np.arange(width)
    one = 2.0 * np.pi * (a[:, None] * p2[None, :] % n_dev) / n_dev
    first = np.concatenate([np.cos(one), -np.sin(one), np.cos(one)[::-1], -np.sin(one)[::-1]])
    two = 2.0 * np.pi * a[:, None] * p1[None, :] / CYCLE_PIX
    turn = np.stack([np.cos(two), np.sin(two), np.cos(two)[::-1], np.sin(two)[::-1]])
    q = np.arange(pairs)
    second = []
    for i in (q, 2 * pairs - 1 - q):
        angle = 2.0 * np.pi * (p1[:, None] * i[None, :] % width) / width
        cos, sin = np.cos(angle), np.sin(angle)
        second.append(np.block([[cos, -sin], [sin, cos]]))
    low = a[:, None] + n_dev * q[None, :]
    half = []
    for m in (low, LMAX - 1 - low):
        angle = np.pi * m / CYCLE_PIX
        cos, sin = np.cos(angle), np.sin(angle)
        half.append(np.concatenate([cos, cos], 1))
        half.append(np.concatenate([sin, -sin], 1))
    f32 = np.float32
    return first.astype(f32), turn.astype(f32), np.stack(second).astype(f32), np.stack(half).astype(f32)


def dft_kernel(
    n_dev, pairs, place_ref, mask_ref, pix_ref, first_ref, turn_ref, second_ref, half_ref, out_ref, x_ref
):
    slots = pix_ref.shape[0]
    cycles = x_ref.shape[0]
    width = CYCLE_PIX // n_dev
    rows = BLOCK_PIX // width
    x_ref[...] = jnp.zeros_like(x_ref)
    for i in range(slots):
        place = place_ref[i]
        cycle, seg = place // SEGS, lax.rem(place, SEGS)
        keep = mask_ref[i].astype(jnp.float32)
        for h in range(rows):
            x_ref[cycle, pl.ds(seg * rows + h, 1), :] = pix_ref[i : i + 1, h * width : (h + 1) * width] * keep
    for phase in range(2):
        for c in range(cycles):
            y = jnp.dot(
                first_ref[2 * phase * n_dev : 2 * (phase + 1) * n_dev, :],
                x_ref[c],
                precision=HIGHEST,
                preferred_element_type=jnp.float32,
            )
            y_re, y_im = y[:n_dev], y[n_dev:]
            cos, sin = turn_ref[2 * phase], turn_ref[2 * phase + 1]
            z = jnp.concatenate([y_re * cos + y_im * sin, y_im * cos - y_re * sin], axis=1)
            spec = jnp.dot(z, second_ref[phase], precision=HIGHEST, preferred_element_type=jnp.float32)
            if c % 2 == 0:
                if 2 * pairs == LANES:
                    swapped = pltpu.roll(spec, pairs, 1)
                else:
                    swapped = jnp.concatenate([spec[:, pairs:], spec[:, :pairs]], axis=1)
                spec = spec * half_ref[2 * phase] + swapped * half_ref[2 * phase + 1]
            out_ref[pl.ds(2 * c + phase, n_dev, stride=2 * cycles), :] = spec


def cycle_spectra(pixels, place, mask, n_dev, cycles):
    pairs = LMAX // (2 * n_dev)
    tables = [jnp.asarray(t) for t in dft_tables(n_dev)]
    smem = pl.BlockSpec(memory_space=pltpu.SMEM)
    vmem = pl.BlockSpec(memory_space=pltpu.VMEM)
    return pl.pallas_call(
        functools.partial(dft_kernel, n_dev, pairs),
        out_shape=jax.ShapeDtypeStruct((n_dev * 2 * cycles, 2 * pairs), jnp.float32),
        in_specs=[smem, smem] + [vmem] * 5,
        out_specs=vmem,
        scratch_shapes=[pltpu.VMEM((cycles, n_dev, CYCLE_PIX // n_dev), jnp.float32)],
        compiler_params=pltpu.CompilerParams(vmem_limit_bytes=32 * 1024 * 1024),
        name="cycle_dft",
    )(place, mask, pixels, *tables)


def wallis(count):
    value = np.zeros(count)
    k = np.arange(0, count - 2, 2)
    value[0::2] = np.concatenate([[1.0], np.cumprod((k + 1.0) / (k + 2.0))])[: len(value[0::2])]
    value[1::2] = 2.0 / np.pi * np.concatenate([[1.0], np.cumprod((k + 2.0) / (k + 3.0))])[: len(value[1::2])]
    return value


def legendre_tables(n_dev, n_blk, cycles_all, slots):
    pairs = LMAX // (2 * n_dev)
    blocks = 2 * pairs + 1
    total = blocks * n_dev
    value = wallis(2 * LMAX + 4 * n_dev + total)
    tau = np.arange(total)[:, None]
    q = (np.arange(LANES) % pairs)[None, :]
    rise = np.where(q < tau // n_dev, tau - n_dev * (q + 1), tau)
    t_rise = value[rise]
    wide = np.arange(total + 2 * n_dev)[:, None]
    t_low = value[np.maximum(wide - n_dev + n_dev * q, 0)]
    t_high = value[wide + 2 * LMAX - 2 - 2 * n_dev * q - 2 * (n_dev - 1)]

    lats = cycles_all // 2
    x = (lats - np.arange(lats)) * (2.0 / (3.0 * NSIDE))
    reps = LANES // pairs
    vregs = lats // (8 * reps)
    order = np.arange(lats).reshape(vregs, reps, 8)
    x_lanes = np.repeat(x[order].transpose(0, 2, 1), pairs, axis=2).reshape(vregs * 8, LANES)
    x_tabs = np.stack([x_lanes, x_lanes * x_lanes, 0.5 * np.log1p(-x_lanes * x_lanes)])

    n_mblk = n_dev // n_blk
    cycle_dev = slots // SEGS
    r_band = cycle_dev * n_mblk
    col = 2 * n_blk * cycle_dev
    pick = np.zeros((4 * lats + 8, n_dev * col))

    def put(row, cycle, phase, weight):
        band, inner = divmod(cycle, r_band)
        j, k = divmod(inner, cycle_dev)
        for s in range(n_blk):
            pick[row, (s * n_mblk + j) * col + (band * cycle_dev + k) * 2 + phase] += weight

    for phase in range(2):
        for n in range(lats):
            for odd in range(2):
                row = (2 * phase + odd) * lats + n
                put(row, n, phase, 1.0)
                if n:
                    put(row, cycles_all - n, phase, -1.0 if odd else 1.0)
        put(4 * lats + phase, lats, phase, 1.0)

    lane = np.arange(LANES)
    band_of = (3 * pairs - 2 - lane) % LANES
    copies = LANES // n_dev
    spread = (band_of[None, :] % copies == (lane // n_dev)[:, None]) & (band_of[None, :] < 2 * pairs)
    gather = band_of[None, :] // copies == np.arange(LMAX // LANES)[:, None]
    f32 = np.float32
    return [t.astype(f32) for t in (t_rise, t_low, t_high, x_tabs, pick, spread, gather)]


def legendre_kernel(
    n_dev,
    pairs,
    lats,
    pixel_total,
    dev_ref,
    got_ref,
    rise_ref,
    low_ref,
    high_ref,
    x_ref,
    pick_ref,
    spread_ref,
    gather_ref,
    out_ref,
    f_ref,
    coef_ref,
    prod_ref,
    accl_ref,
    acch_ref,
):
    d = dev_ref[0]
    reps = LANES // pairs
    vregs = lats // (8 * reps)
    blocks = 2 * pairs + 1
    tiles = n_dev // 8
    group = min(4, tiles)
    span = 2 * pairs

    lane = lax.broadcasted_iota(jnp.int32, (8, LANES), 1)
    sub = lax.broadcasted_iota(jnp.int32, (8, LANES), 0)
    q = lane % pairs
    m_low = (d + n_dev * q).astype(jnp.float32)
    m_high = (LMAX - 1.0) - m_low

    f_all = jnp.dot(pick_ref[...], got_ref[...], precision=HIGHEST, preferred_element_type=jnp.float32)

    def lanes_of(start, v, part):
        pieces = []
        for h in range(reps):
            row = start + (v * reps + h) * 8
            pieces.append(f_all[row : row + 8, part * pairs : (part + 1) * pairs])
        return jnp.concatenate(pieces, axis=1)

    for phase in range(2):
        for odd in range(2):
            for v in range(vregs):
                for part in range(2):
                    val = lanes_of((2 * phase + odd) * lats, v, part)
                    if odd:
                        val = val * x_ref[0, 8 * v : 8 * v + 8, :]
                    slot = ((phase * 2 + odd) * vregs + v) * 2 + part
                    f_ref[8 * slot : 8 * slot + 8, :] = val
    base = 8 * vregs
    for phase in range(2):
        for part in range(2):
            row = f_all[4 * lats + phase : 4 * lats + phase + 1, part * pairs : (part + 1) * pairs]
            row = jnp.concatenate([row] * reps, axis=1)
            slot = base + phase * 2 + part
            f_ref[8 * slot : 8 * slot + 8, :] = jnp.broadcast_to(row, (8, LANES))

    accl_ref[...] = jnp.zeros_like(accl_ref)
    acch_ref[...] = jnp.zeros_like(acch_ref)
    x2 = [x_ref[1, 8 * v : 8 * v + 8, :] for v in range(vregs)]
    logs = [x_ref[2, 8 * v : 8 * v + 8, :] for v in range(vregs)]
    seed_low = [jnp.exp(m_low * g) for g in logs]
    seed_high = [jnp.exp(m_high * g) for g in logs]
    sign = jnp.where(sub % 4 == 0, 1.0, jnp.where(sub % 4 == 2, -1.0, 0.0)).astype(jnp.float32)
    q_f = q.astype(jnp.float32)
    sub_f = sub.astype(jnp.float32)
    d_f = d.astype(jnp.float32)
    weight_low = jnp.where(m_low == 0.0, 1.0, 2.0) / pixel_total
    weight_high = jnp.full((8, LANES), 2.0 / pixel_total, jnp.float32)
    head = lane < pairs

    def one_block(b, state):
        even, odd = list(state[:vregs]), list(state[vregs:])
        is_low = q < b
        turned = q == b - 1
        even = [jnp.where(turned, s, e) for s, e in zip(seed_low, even)]
        odd = [jnp.where(turned, 0.0, o) for o in odd]

        def pick_phase(slot_low, slot_high):
            return jnp.where(is_low, f_ref[8 * slot_low : 8 * slot_low + 8, :], f_ref[8 * slot_high : 8 * slot_high + 8, :])

        def spectra(parity, v, part):
            return pick_phase((parity * vregs + v) * 2 + part, ((2 + parity) * vregs + v) * 2 + part)

        f_now = [[[spectra(o, v, part) for part in range(2)] for v in range(vregs)] for o in range(2)]
        flat = [pick_phase(base + part, base + 2 + part) * sign for part in range(2)]
        weight = jnp.where(is_low, weight_low, weight_high)
        start = (b * n_dev).astype(jnp.float32)
        l_first = jnp.where(is_low, start - n_dev + d_f, start + (LMAX - 1.0) - d_f - n_dev * q_f) + sub_f
        low_lane = jnp.logical_and(head, is_low)
        high_lane = jnp.logical_and(head, jnp.logical_not(is_low))
        target = lax.rem(3 * pairs - 2 - (b - 1) + 2 * LANES, LANES)

        def one_group(g, state):
            even, odd = list(state[:vregs]), list(state[vregs:])
            weights = []
            for i in range(group):
                row = g * (8 * group) + 8 * i
                tau = b * n_dev + row
                vv = rise_ref[pl.ds(pl.multiple_of(tau, 8), 8), :] * jnp.where(
                    is_low, low_ref[pl.ds(tau + 2 * d, 8), :], high_ref[pl.ds(tau + 2 * (n_dev - 1 - d), 8), :]
                )
                degree = l_first + lax.convert_element_type(row, jnp.float32)
                coef_ref[8 * i : 8 * i + 8, :] = vv * (degree * math.pi + 0.5 * math.pi)
                weights.append(jnp.where(degree < LMAX, vv * weight, 0.0))
            for i in range(group):
                for j in range(0, 8, 2):
                    for parity in range(2):
                        step = 8 * i + j + parity
                        now = odd if parity else even
                        for part in range(2):
                            total = now[0] * f_now[parity][0][part]
                            for v in range(1, vregs):
                                total = total + now[v] * f_now[parity][v][part]
                            prod_ref[part, 8 * step : 8 * step + 8, :] = total
                        coef = coef_ref[step : step + 1, :]
                        if parity:
                            even = [(coef * x2[v]) * odd[v] - even[v] for v in range(vregs)]
                        else:
                            odd = [coef * even[v] - odd[v] for v in range(vregs)]
                sums = []
                for part in range(2):
                    total = prod_ref[part, pl.ds(64 * i, 8, stride=8), :]
                    for s in range(1, 8):
                        total = total + prod_ref[part, pl.ds(64 * i + s, 8, stride=8), :]
                    width = pairs
                    while width < LANES:
                        total = total + pltpu.roll(total, width, 1)
                        width *= 2
                    sums.append(total + flat[part])
                power = (sums[0] * sums[0] + sums[1] * sums[1]) * weights[i]
                row = pl.multiple_of(g * (8 * group) + 8 * i, 8)
                low_sum = jnp.sum(jnp.where(low_lane, power, 0.0), axis=1, keepdims=True)
                accl_ref[pl.ds(row, 8), :] = jnp.where(lane == target, low_sum, accl_ref[pl.ds(row, 8), :])

                @pl.when(b < pairs)
                def _():
                    acch_ref[pl.ds(row, 8), :] = pltpu.roll(acch_ref[pl.ds(row, 8), :], 1, 1) + jnp.where(
                        high_lane, power, 0.0
                    )

            return (*even, *odd)

        if tiles == group:
            return one_group(0, (*even, *odd))
        return lax.fori_loop(0, tiles // group, one_group, (*even, *odd))

    zero = jnp.zeros((8, LANES), jnp.float32)
    lax.fori_loop(0, blocks, one_block, (*seed_high, *([zero] * vregs)))

    rows = lax.broadcasted_iota(jnp.int32, (n_dev, LANES), 0)

    def shifted(acc, shift):
        rolled = pltpu.roll(acc, shift, 0)
        return jnp.where(rows < shift, pltpu.roll(rolled, LANES - 1, 1), rolled)

    power = shifted(accl_ref[...], d) + shifted(acch_ref[...], n_dev - 1 - d)
    copies = LANES // n_dev
    tall = jnp.concatenate([power] * copies, axis=0) * spread_ref[...]
    out_ref[...] = lax.dot_general(
        gather_ref[...], tall, (((1,), (1,)), ((), ())), precision=HIGHEST, preferred_element_type=jnp.float32
    )


def legendre_power(got, dev, n_dev, n_blk, cycles_all, slots):
    pairs = LMAX // (2 * n_dev)
    lats = cycles_all // 2
    vregs = lats * pairs // (8 * LANES)
    tables = [jnp.asarray(t) for t in legendre_tables(n_dev, n_blk, cycles_all, slots)]
    smem = pl.BlockSpec(memory_space=pltpu.SMEM)
    vmem = pl.BlockSpec(memory_space=pltpu.VMEM)
    return pl.pallas_call(
        functools.partial(legendre_kernel, n_dev, pairs, lats, float(cycles_all * CYCLE_PIX)),
        out_shape=jax.ShapeDtypeStruct((LMAX // LANES, LANES), jnp.float32),
        in_specs=[smem] + [vmem] * 8,
        out_specs=vmem,
        scratch_shapes=[
            pltpu.VMEM((8 * (8 * vregs + 4), LANES), jnp.float32),
            pltpu.VMEM((32, LANES), jnp.float32),
            pltpu.VMEM((2, 256, LANES), jnp.float32),
            pltpu.VMEM((n_dev, LANES), jnp.float32),
            pltpu.VMEM((n_dev, LANES), jnp.float32),
        ],
        compiler_params=pltpu.CompilerParams(vmem_limit_bytes=48 * 1024 * 1024),
        name="legendre_power",
    )(dev, got, *tables)


def on_device(pixels, block_ids, block_mask, model_cl):
    n_blk = lax.axis_size("blk")
    n_mblk = lax.axis_size("mblk")
    n_dev = n_blk * n_mblk
    both = ("blk", "mblk")
    dev = lax.axis_index("blk") * n_mblk + lax.axis_index("mblk")
    slots = pixels.shape[0]
    cycle_dev = slots // SEGS
    cycles = n_blk * cycle_dev
    r_band = cycle_dev * n_mblk
    cycles_all = r_band * n_blk
    pairs = LMAX // (2 * n_dev)

    cycle = block_ids // SEGS
    band = cycle // r_band
    local = cycle - band * r_band - lax.axis_index("mblk") * cycle_dev
    place = (band * cycle_dev + local) * SEGS + block_ids % SEGS
    sent = cycle_spectra(pixels, place, block_mask, n_dev, cycles)
    got = lax.all_to_all(sent.reshape(n_dev, 2 * cycles, 2 * pairs), both, 0, 0, tiled=True)
    got = got.reshape(n_dev * 2 * cycles, 2 * pairs)
    power = legendre_power(got, dev[None], n_dev, n_blk, cycles_all, slots)

    bit = 1
    while bit < n_mblk:
        power = power + lax.ppermute(power, "mblk", [(i, i ^ bit) for i in range(n_mblk)])
        bit *= 2
    bit = 1
    while bit < n_blk:
        power = power + lax.ppermute(power, "blk", [(i, i ^ bit) for i in range(n_blk)])
        bit *= 2
    pseudo_cl = power.reshape(LMAX)
    rel_error = (pseudo_cl - model_cl) / model_cl
    misfit = jnp.mean(rel_error * rel_error)
    return (pseudo_cl, misfit)


def solution(mesh):
    in_specs = (P(("blk", "mblk"), None), P(("blk", "mblk")), P(("blk", "mblk")), P())
    out_specs = (P(), P())
    return jax.shard_map(
        on_device, mesh=mesh, in_specs=in_specs, out_specs=out_specs, check_vma=False
    )
```

```python
import functools
import math

import jax
import jax.numpy as jnp
import numpy as np
from jax import lax
from jax.experimental import pallas as pl
from jax.experimental.pallas import tpu as pltpu
from jax.sharding import PartitionSpec as P

NSIDE = 2048
CYCLE_PIX = 8192
LMAX = 4096
BLOCK_PIX = 1024
SEGS = 8
LANES = 128
CHUNK = 32
PITCH = 12
STREAMED = 80
PIECES = 5
VMEM_LIMIT = 56 * 1024 * 1024
F32 = jnp.float32
BF16 = jnp.bfloat16
ANY = pl.BlockSpec(memory_space=pl.ANY)
SMEM = pl.BlockSpec(memory_space=pltpu.SMEM)
VMEM = pl.BlockSpec(memory_space=pltpu.VMEM)


def device_index():
    return lax.axis_index("blk") * lax.axis_size("mblk") + lax.axis_index("mblk")


def split_table(table):
    high = table.astype(jnp.bfloat16)
    low = (table - high.astype(np.float64)).astype(jnp.bfloat16)
    return high, low


def split(x):
    high = x.astype(BF16)
    return high, (x - high.astype(F32)).astype(BF16)


def dot(a, b):
    return jnp.dot(a, b, preferred_element_type=F32)


def fetch(pairs, sems):
    copies = [pltpu.make_async_copy(src, dst, sems.at[i]) for i, (src, dst) in enumerate(pairs)]
    for copy in copies:
        copy.start()
    return copies


def dft_tables(n_dev):
    width = CYCLE_PIX // n_dev
    pairs = LMAX // (2 * n_dev)
    a = np.arange(n_dev)
    p2 = np.arange(n_dev)
    p1 = np.arange(width)
    one = 2.0 * np.pi * (a[:, None] * p2[None, :] % n_dev) / n_dev
    first = np.concatenate([np.cos(one), -np.sin(one), np.cos(one)[::-1], -np.sin(one)[::-1]])
    high, low = split_table(first)
    first = np.concatenate([high, low, high], axis=1)
    two = 2.0 * np.pi * a[:, None] * p1[None, :] / CYCLE_PIX
    turn = np.stack([np.cos(two), np.sin(two), np.cos(two)[::-1], np.sin(two)[::-1]])
    q = np.arange(pairs)
    second = []
    for i in (q, 2 * pairs - 1 - q):
        angle = 2.0 * np.pi * (p1[:, None] * i[None, :] % width) / width
        cos, sin = np.cos(angle), np.sin(angle)
        second.append(np.concatenate(split_table(np.block([[cos, -sin], [sin, cos]])), axis=1))
    below = a[:, None] + n_dev * q[None, :]
    half = []
    for m in (below, LMAX - 1 - below):
        angle = np.pi * m / CYCLE_PIX
        cos, sin = np.cos(angle), np.sin(angle)
        half.append(np.concatenate([cos, cos], 1))
        half.append(np.concatenate([sin, -sin], 1))
    return first, turn.astype(np.float32), np.stack(second), np.stack(half).astype(np.float32)


def dft_kernel(
    n_dev,
    n_blk,
    ids_ref,
    mask_ref,
    pix_hbm,
    first_hbm,
    turn_hbm,
    second_hbm,
    half_hbm,
    out_ref,
    x_ref,
    pix_ref,
    first_ref,
    turn_ref,
    second_ref,
    half_ref,
    sems,
):
    copies = fetch(
        [
            (pix_hbm, pix_ref),
            (first_hbm, first_ref),
            (turn_hbm, turn_ref),
            (second_hbm, second_ref),
            (half_hbm, half_ref),
        ],
        sems,
    )
    slots = pix_ref.shape[0]
    cycle_dev = slots // SEGS
    cycles = n_blk * cycle_dev
    r_band = cycle_dev * (n_dev // n_blk)
    own = lax.axis_index("mblk") * cycle_dev
    width = CYCLE_PIX // n_dev
    rows = BLOCK_PIX // width
    pairs = LMAX // (2 * n_dev)
    x_ref[...] = jnp.zeros_like(x_ref)
    copies[0].wait()
    for i in range(slots):
        number = ids_ref[i]
        cycle, seg = lax.div(number, SEGS), lax.rem(number, SEGS)
        band = lax.div(cycle, r_band)
        place = band * cycle_dev + cycle - band * r_band - own
        keep = mask_ref[i].astype(F32)
        for h in range(rows):
            x_ref[place, pl.ds(seg * rows + h, 1), :] = pix_ref[i : i + 1, h * width : (h + 1) * width] * keep
    x = jnp.concatenate([x_ref[c] for c in range(cycles)], axis=1)
    x_high, x_low = split(x)
    copies[1].wait()
    y = dot(first_ref[...], jnp.concatenate([x_high, x_high, x_low], axis=0))
    copies[2].wait()
    copies[3].wait()
    copies[4].wait()
    for phase in range(2):
        y_re = y[2 * phase * n_dev : (2 * phase + 1) * n_dev]
        y_im = y[(2 * phase + 1) * n_dev : (2 * phase + 2) * n_dev]
        cos, sin = turn_ref[2 * phase], turn_ref[2 * phase + 1]
        z = []
        for c in range(cycles):
            re, im = y_re[:, c * width : (c + 1) * width], y_im[:, c * width : (c + 1) * width]
            z.append(jnp.concatenate([re * cos + im * sin, im * cos - re * sin], axis=1))
        z_high, z_low = split(jnp.concatenate(z, axis=0))
        table = second_ref[phase]
        both = dot(z_high, table)
        spec_all = both[:, : 2 * pairs] + both[:, 2 * pairs :] + dot(z_low, table[:, : 2 * pairs])
        for c in range(cycles):
            spec = spec_all[c * n_dev : (c + 1) * n_dev]
            if c % 2 == 0:
                if 2 * pairs == LANES:
                    swapped = pltpu.roll(spec, pairs, 1)
                else:
                    swapped = jnp.concatenate([spec[:, pairs:], spec[:, :pairs]], axis=1)
                spec = spec * half_ref[2 * phase] + swapped * half_ref[2 * phase + 1]
            out_ref[pl.ds(2 * c + phase, n_dev, stride=2 * cycles), :] = spec


def cycle_spectra(pixels, block_ids, mask, n_dev, n_blk):
    pairs = LMAX // (2 * n_dev)
    cycles = n_blk * pixels.shape[0] // SEGS
    tables = [jnp.asarray(t) for t in dft_tables(n_dev)]
    return pl.pallas_call(
        functools.partial(dft_kernel, n_dev, n_blk),
        out_shape=jax.ShapeDtypeStruct((n_dev * 2 * cycles, 2 * pairs), F32),
        in_specs=[SMEM, SMEM] + [ANY] * 5,
        out_specs=VMEM,
        scratch_shapes=[pltpu.VMEM((cycles, n_dev, CYCLE_PIX // n_dev), F32), pltpu.VMEM(pixels.shape, F32)]
        + [pltpu.VMEM(t.shape, t.dtype) for t in tables]
        + [pltpu.SemaphoreType.DMA((5,))],
        compiler_params=pltpu.CompilerParams(vmem_limit_bytes=VMEM_LIMIT),
        name="cycle_dft",
    )(block_ids, mask, pixels, *tables)


def wallis(count):
    value = np.zeros(count)
    k = np.arange(0, count - 2, 2)
    value[0::2] = np.concatenate([[1.0], np.cumprod((k + 1.0) / (k + 2.0))])[: len(value[0::2])]
    value[1::2] = 2.0 / np.pi * np.concatenate([[1.0], np.cumprod((k + 2.0) / (k + 3.0))])[: len(value[1::2])]
    return value


def step_blocks(n_dev):
    blocks = LMAX // n_dev + 1
    return blocks + blocks * (n_dev // CHUNK) % 2


def latitude_lanes(n_dev, lats):
    pairs = LMAX // (2 * n_dev)
    x = (lats - np.arange(lats)) * (2.0 / (3.0 * NSIDE))
    reps = LANES // pairs
    order = np.arange(lats).reshape(-1, reps, 8)
    return np.repeat(x[order].transpose(0, 2, 1), pairs, axis=2).reshape(-1, LANES)


def recurrence_tables(n_dev, lats):
    pairs = LMAX // (2 * n_dev)
    total = step_blocks(n_dev) * n_dev
    value = wallis(2 * LMAX + 6 * n_dev + total)
    tau = np.arange(total)[:, None]
    q = np.arange(pairs)[None, :]
    rise = np.where(q < tau // n_dev, tau - n_dev * (q + 1), tau)
    wide = np.arange(total + 2 * n_dev)[:, None]
    t_low = value[np.maximum(wide - n_dev + n_dev * q, 0)]
    t_high = value[wide + 2 * LMAX - 2 - 2 * n_dev * q - 2 * (n_dev - 1)]
    x = latitude_lanes(n_dev, lats)
    x_tabs = np.stack([x, x * x, 0.5 * np.log1p(-x * x)])
    tables = [np.tile(t, (1, LANES // pairs)) for t in (value[rise], t_low, t_high)]
    return [t.astype(np.float32) for t in tables + [x_tabs]]


def advance(coef_ref, row, even, odd, x2):
    one, two = coef_ref[pl.ds(row, 1), :], coef_ref[pl.ds(row + 1, 1), :]
    fresh_odd = [one * e - o for e, o in zip(even, odd)]
    gains = [two * x for x in x2]
    fresh_even = [(g * one - 1.0) * e - g * o for g, e, o in zip(gains, even, odd)]
    return fresh_even, fresh_odd


def turn_lanes(chunk, per_block, q, seeds, even, odd):
    turned = q == lax.div(chunk, per_block) - 1
    if per_block > 1:
        turned = jnp.logical_and(turned, lax.rem(chunk, per_block) == 0)
    return [jnp.where(turned, s, e) for s, e in zip(seeds, even)], [jnp.where(turned, 0.0, o) for o in odd]


def recurrence_kernel(
    n_dev,
    vregs,
    pixel_total,
    rise_hbm,
    low_hbm,
    high_hbm,
    x_hbm,
    rows_hbm,
    u_hbm,
    rise_ref,
    low_ref,
    high_ref,
    x_ref,
    rows_ref,
    u_ref,
    sems,
):
    copies = fetch([(rise_hbm, rise_ref), (low_hbm, low_ref), (high_hbm, high_ref), (x_hbm, x_ref)], sems)
    d = device_index()
    pairs = LMAX // (2 * n_dev)
    per_block = n_dev // CHUNK
    chunks = step_blocks(n_dev) * per_block
    inline = chunks - STREAMED
    total = chunks * CHUNK
    many = max(n for n in range(1, 13) if chunks % n == 0)
    lane = lax.broadcasted_iota(jnp.int32, (8, LANES), 1)
    sub = lax.broadcasted_iota(jnp.int32, (8, LANES), 0)
    q = lax.rem(lane, pairs)
    m_low = (d + n_dev * q).astype(F32)
    m_high = (LMAX - 1.0) - m_low
    weight_low = jnp.where(m_low == 0.0, 1.0, 2.0) / pixel_total
    weight_high = jnp.full((8, LANES), 2.0 / pixel_total, F32)
    l_low = sub.astype(F32) + (d.astype(F32) - n_dev)
    l_high = sub.astype(F32) + m_high
    for copy in copies:
        copy.wait()
    x2 = [x_ref[1, 8 * v : 8 * v + 8, :] for v in range(vregs)]
    logs = [x_ref[2, 8 * v : 8 * v + 8, :] for v in range(vregs)]
    seed_low = [jnp.exp(m_low * g) for g in logs]
    seed_high = [jnp.exp(m_high * g) for g in logs]

    def coefficients(first, carry):
        fresh = []
        for step in range(many):
            chunk = first * many + step
            is_low = q < lax.div(chunk, per_block)
            weight = jnp.where(is_low, weight_low, weight_high)
            start = jnp.where(is_low, l_low, l_high) + (chunk * CHUNK).astype(F32)
            for i in range(CHUNK // 8):
                tau = pl.multiple_of(chunk * CHUNK, CHUNK) + 8 * i
                low = low_ref[pl.ds(tau + 2 * d, 8), :]
                high = high_ref[pl.ds(tau + 2 * (n_dev - 1 - d), 8), :]
                product = rise_ref[pl.ds(tau, 8), :] * jnp.where(is_low, low, high)
                degree = start + 8.0 * i
                coef = product * (degree * math.pi + 0.5 * math.pi)
                fresh.append((tau, coef, jnp.where(degree < LMAX, product * weight, 0.0)))
        for tau, coef, weight in fresh:
            rows_ref[pl.ds(tau, 8), :] = coef
            rows_ref[pl.ds(total + tau, 8), :] = weight
        return carry

    def steps(chunk, state):
        even, odd = turn_lanes(chunk, per_block, q, seed_low, list(state[:vregs]), list(state[vregs:]))
        first = pl.multiple_of(chunk * CHUNK, CHUNK)
        start = pl.multiple_of((chunk - inline) * (CHUNK * 8 * vregs), CHUNK * 8 * vregs)
        for s in range(0, CHUNK, 2):
            fresh_even, fresh_odd = advance(rows_ref, first + s, even, odd, x2)
            for v in range(vregs):
                u_ref[pl.ds(start + 8 * (s * vregs + v), 8), :] = even[v]
                u_ref[pl.ds(start + 8 * ((s + 1) * vregs + v), 8), :] = fresh_odd[v]
            even, odd = fresh_even, fresh_odd
        return (*even, *odd)

    def plain_steps(chunk, state):
        even, odd = turn_lanes(chunk, per_block, q, seed_low, list(state[:vregs]), list(state[vregs:]))
        first = pl.multiple_of(chunk * CHUNK, CHUNK)
        for s in range(0, CHUNK, 2):
            even, odd = advance(rows_ref, first + s, even, odd, x2)
        return (*even, *odd)

    lax.fori_loop(0, chunks // many, coefficients, 0)
    out = [pltpu.make_async_copy(rows_ref, rows_hbm, sems.at[4])]
    out[0].start()
    zero = jnp.zeros((8, LANES), F32)
    state = (*seed_high, *([zero] * vregs))
    state = lax.fori_loop(0, inline // 2, lambda h, s: plain_steps(2 * h + 1, plain_steps(2 * h, s)), state)
    piece = STREAMED // PIECES
    for p in range(PIECES):
        first = inline + p * piece
        state = lax.fori_loop(first // 2, (first + piece) // 2, lambda h, s: steps(2 * h + 1, steps(2 * h, s)), state)
        size = piece * CHUNK * 8 * vregs
        out.append(pltpu.make_async_copy(u_ref.at[pl.ds(p * size, size)], u_hbm.at[pl.ds(p * size, size)], sems.at[5 + p]))
        out[-1].start()
    for copy in out:
        copy.wait()


def legendre_rows(n_dev, lats):
    pairs = LMAX // (2 * n_dev)
    vregs = lats * pairs // (8 * LANES)
    total = step_blocks(n_dev) * n_dev
    tables = [jnp.asarray(t) for t in recurrence_tables(n_dev, lats)]
    rows = jax.ShapeDtypeStruct((2 * total, LANES), F32)
    u = jax.ShapeDtypeStruct((STREAMED * CHUNK * 8 * vregs, LANES), F32)
    return pl.pallas_call(
        functools.partial(recurrence_kernel, n_dev, vregs, float(2 * lats * CYCLE_PIX)),
        out_shape=(rows, u),
        in_specs=[ANY] * 4,
        out_specs=(ANY, ANY),
        scratch_shapes=[pltpu.VMEM(t.shape, t.dtype) for t in [*tables, rows, u]]
        + [pltpu.SemaphoreType.DMA((5 + PIECES,))],
        compiler_params=pltpu.CompilerParams(vmem_limit_bytes=VMEM_LIMIT),
        cost_estimate=pl.CostEstimate(flops=total * 8 * LANES * vregs * 8, bytes_accessed=30000000, transcendentals=0),
        name="legendre_rows",
    )(*tables)


def power_tables(n_dev, n_blk, lats, slots):
    pairs = LMAX // (2 * n_dev)
    cycles_all = 2 * lats
    n_mblk = n_dev // n_blk
    cycle_dev = slots // SEGS
    r_band = cycle_dev * n_mblk
    col = 2 * n_blk * cycle_dev
    pick = np.zeros((4 * lats + 16, n_dev * col))

    def put(row, cycle, phase, weight):
        band, inner = divmod(cycle, r_band)
        j, k = divmod(inner, cycle_dev)
        for s in range(n_blk):
            pick[row, (s * n_mblk + j) * col + (band * cycle_dev + k) * 2 + phase] += weight

    for phase in range(2):
        for n in range(lats):
            for odd in range(2):
                row = (2 * phase + odd) * lats + n
                put(row, n, phase, 1.0)
                if n:
                    put(row, cycles_all - n, phase, -1.0 if odd else 1.0)
        put(4 * lats + phase, lats, phase, 1.0)

    lane = np.arange(LANES)
    band_of = (3 * pairs - 2 - lane) % LANES
    copies = LANES // n_dev
    spread = (band_of[None, :] % copies == (lane // n_dev)[:, None]) & (band_of[None, :] < 2 * pairs)
    gather = band_of[None, :] // copies == np.arange(LMAX // LANES)[:, None]
    return (
        pick.astype(jnp.bfloat16),
        recurrence_tables(n_dev, lats)[3],
        spread.astype(np.float32),
        gather.astype(jnp.bfloat16),
    )


def exact_dot(zero_one, x, dims):
    total = None
    for _ in range(3):
        part = x.astype(BF16)
        x = x - part.astype(F32)
        term = lax.dot_general(zero_one, part, (dims, ((), ())), preferred_element_type=F32)
        total = term if total is None else total + term
    return total


def power_kernel(
    n_dev,
    vregs,
    rows_hbm,
    u_hbm,
    got_hbm,
    pick_hbm,
    x_hbm,
    spread_hbm,
    gather_hbm,
    out_ref,
    rows_ref,
    u_ref,
    got_ref,
    pick_ref,
    x_ref,
    spread_ref,
    gather_ref,
    f_ref,
    prod_a,
    prod_b,
    sum_ref,
    accl_ref,
    acch_ref,
    sems,
):
    small = [
        (got_hbm, got_ref),
        (pick_hbm, pick_ref),
        (x_hbm, x_ref),
        (rows_hbm, rows_ref),
        (spread_hbm, spread_ref),
        (gather_hbm, gather_ref),
    ]
    size = u_ref.shape[0] // PIECES
    large = [(u_hbm.at[pl.ds(p * size, size)], u_ref.at[pl.ds(p * size, size)]) for p in range(PIECES)]
    copies = fetch(small + large, sems)
    d = device_index()
    pairs = LMAX // (2 * n_dev)
    reps = LANES // pairs
    lats = vregs * 8 * reps
    per_block = n_dev // CHUNK
    blocks = step_blocks(n_dev)
    chunks = blocks * per_block
    inline = chunks - STREAMED
    weights = chunks * CHUNK
    lane = lax.broadcasted_iota(jnp.int32, (8, LANES), 1)
    sub = lax.broadcasted_iota(jnp.int32, (8, LANES), 0)
    q = lax.rem(lane, pairs)
    head = lane < pairs
    sign = jnp.where(sub % 4 == 0, 1.0, jnp.where(sub % 4 == 2, -1.0, 0.0)).astype(F32)
    accl_ref[...] = jnp.zeros_like(accl_ref)
    acch_ref[...] = jnp.zeros_like(acch_ref)
    prod_b[...] = jnp.zeros_like(prod_b)

    for copy in copies[:3]:
        copy.wait()
    f_all = exact_dot(pick_ref[...], got_ref[...], ((1,), (0,)))

    def store(slot, value):
        f_ref[8 * slot : 8 * slot + 8, :] = value

    def load(slot):
        return f_ref[8 * slot : 8 * slot + 8, :]

    for phase in range(2):
        for odd in range(2):
            for v in range(vregs):
                for part in range(2):
                    pieces = []
                    for h in range(reps):
                        row = (2 * phase + odd) * lats + (v * reps + h) * 8
                        pieces.append(f_all[row : row + 8, part * pairs : (part + 1) * pairs])
                    value = jnp.concatenate(pieces, axis=1)
                    if odd:
                        value = value * x_ref[0, 8 * v : 8 * v + 8, :]
                    store(((phase * 2 + odd) * vregs + v) * 2 + part, value)
    base = 8 * vregs
    for phase in range(2):
        row = f_all[4 * lats + phase : 4 * lats + phase + 1, :]
        if 2 * pairs < LANES:
            row = jnp.concatenate([row, jnp.zeros((1, LANES - 2 * pairs), F32)], axis=1)
        store(base + phase, jnp.broadcast_to(row, (8, LANES)) * sign)

    def spectra_now(chunk):
        is_low = q < lax.div(chunk, per_block)

        def now(o, v, p):
            return jnp.where(is_low, load((o * vregs + v) * 2 + p), load(((2 + o) * vregs + v) * 2 + p))

        return [[[now(o, v, p) for p in range(2)] for v in range(vregs)] for o in range(2)]

    def product(s, u, now, prod_ref):
        for part in range(2):
            value = u[0] * now[s % 2][0][part]
            for v in range(1, vregs):
                value = value + u[v] * now[s % 2][v][part]
            prod_ref[part, pl.ds((s // 8) * 8 * PITCH + s % 8, 8, stride=PITCH), :] = value

    def products(chunk, prod_ref):
        now = spectra_now(chunk)
        start = pl.multiple_of((chunk - inline) * (CHUNK * 8 * vregs), CHUNK * 8 * vregs)
        for s in range(CHUNK):
            product(s, [u_ref[pl.ds(start + 8 * (s * vregs + v), 8), :] for v in range(vregs)], now, prod_ref)

    def steps(chunk, prod_ref, state):
        now = spectra_now(chunk)
        even, odd = turn_lanes(chunk, per_block, q, seed_low, list(state[:vregs]), list(state[vregs:]))
        first = pl.multiple_of(chunk * CHUNK, CHUNK)
        for s in range(0, CHUNK, 2):
            fresh_even, fresh_odd = advance(rows_ref, first + s, even, odd, x2)
            product(s, even, now, prod_ref)
            product(s + 1, fresh_odd, now, prod_ref)
            even, odd = fresh_even, fresh_odd
        return (*even, *odd)

    def reduce(chunk, prod_ref):
        for i in range(CHUNK // 8):
            for part in range(2):
                rows = [prod_ref[part, pl.ds((8 * i + s) * PITCH, 8), :] for s in range(8)]
                while len(rows) > 1:
                    rows = [a + b for a, b in zip(rows[::2], rows[1::2])]
                sum_ref[part, pl.ds(pl.multiple_of(chunk * CHUNK, CHUNK) + 8 * i, 8), :] = rows[0]

    def two_inline(h, state):
        state = steps(2 * h, prod_a, state)
        reduce(jnp.maximum(2 * h - 1, 0), prod_b)
        state = steps(2 * h + 1, prod_b, state)
        reduce(2 * h, prod_a)
        return state

    def two_streamed(h, carry):
        products(2 * h, prod_a)
        reduce(2 * h - 1, prod_b)
        products(2 * h + 1, prod_b)
        reduce(2 * h, prod_a)
        return carry

    m_low = (d + n_dev * q).astype(F32)
    x2 = [x_ref[1, 8 * v : 8 * v + 8, :] for v in range(vregs)]
    logs = [x_ref[2, 8 * v : 8 * v + 8, :] for v in range(vregs)]
    seed_low = [jnp.exp(m_low * g) for g in logs]
    seed_high = [jnp.exp(((LMAX - 1.0) - m_low) * g) for g in logs]
    for copy in copies[3:6]:
        copy.wait()
    lax.fori_loop(0, inline // 2, two_inline, (*seed_high, *([jnp.zeros((8, LANES), F32)] * vregs)))
    piece = STREAMED // PIECES
    for p in range(PIECES):
        copies[6 + p].wait()
        first = inline + p * piece
        lax.fori_loop(first // 2, (first + piece) // 2, two_streamed, 0)
    reduce(chunks - 1, prod_b)

    def packed(tau):
        re, im = sum_ref[0, pl.ds(tau, 8), :], sum_ref[1, pl.ds(tau, 8), :]
        if 2 * pairs == LANES:
            return jnp.where(head, re, im) + pltpu.roll(jnp.where(head, im, re), pairs, 1)
        step = pairs
        while step < LANES:
            re, im = re + pltpu.roll(re, step, 1), im + pltpu.roll(im, step, 1)
            step *= 2
        return jnp.where(head, re, jnp.where(lane < 2 * pairs, im, 0.0))

    def powers(first, count, with_high):
        tiles = n_dev // 8
        places = [(i, j) for j in range(count) for i in range(tiles)]
        taus = [pl.multiple_of((first + j) * n_dev, n_dev) + 8 * i for i, j in places]
        lows = [q < first + j for j in range(count)]
        flats = [load(base)] * count
        if with_high:
            flats = [jnp.where(low, load(base), load(base + 1)) for low in lows]
        values = [packed(tau) for tau in taus]
        values = [v + flats[j] for v, (_, j) in zip(values, places)]
        values = [v * v * rows_ref[pl.ds(weights + tau, 8), :] for v, tau in zip(values, taus)]
        low_parts = values
        if with_high:
            low_parts = [jnp.where(lows[j], v, 0.0) for v, (_, j) in zip(values, places)]
            high_parts = [v - low for v, low in zip(values, low_parts)]
        sums = [jnp.sum(v, axis=1, keepdims=True) for v in low_parts]
        if with_high:
            shifts = [count - 1 - j for _, j in places]
            high_parts = [pltpu.roll(v, shift, 1) if shift else v for v, shift in zip(high_parts, shifts)]
        for i in range(tiles):
            total = accl_ref[8 * i : 8 * i + 8, :]
            for j in range(count):
                target = lax.rem(3 * pairs - 1 - (first + j) + 2 * LANES, LANES)
                total = total + jnp.where(lane == target, sums[j * tiles + i], 0.0)
            accl_ref[8 * i : 8 * i + 8, :] = total
            if with_high:
                total = pltpu.roll(acch_ref[8 * i : 8 * i + 8, :], count, 1)
                for j in range(count):
                    total = total + high_parts[j * tiles + i]
                acch_ref[8 * i : 8 * i + 8, :] = total

    many = 512 // n_dev
    half = pairs // many

    def both_halves(g, carry):
        powers(g * many, many, True)
        return carry

    def low_half(g, carry):
        powers(g * many, many, False)
        return carry

    lax.fori_loop(0, half, both_halves, 0)
    lax.fori_loop(half, blocks // many, low_half, 0)
    if blocks % many:
        powers(jnp.int32(blocks - blocks % many), blocks % many, False)

    rows = lax.broadcasted_iota(jnp.int32, (n_dev, LANES), 0)

    def shifted(acc, shift):
        rolled = pltpu.roll(acc, shift, 0)
        return jnp.where(rows < shift, pltpu.roll(rolled, LANES - 1, 1), rolled)

    lanes = lax.broadcasted_iota(jnp.int32, (n_dev, LANES), 1)
    high = acch_ref[...] + pltpu.roll(acch_ref[...], LANES - pairs, 1)
    high = jnp.where(jnp.logical_and(lanes >= pairs - 1, lanes < 2 * pairs - 1), high, 0.0)
    power = shifted(accl_ref[...], d) + shifted(high, n_dev - 1 - d)
    tall = jnp.concatenate([power] * (LANES // n_dev), axis=0) * spread_ref[...]
    out_ref[...] = exact_dot(gather_ref[...], tall, ((1,), (1,)))


def power_of_orders(rows, u, got, n_dev, n_blk, lats, slots):
    pairs = LMAX // (2 * n_dev)
    vregs = lats * pairs // (8 * LANES)
    tables = [jnp.asarray(t) for t in power_tables(n_dev, n_blk, lats, slots)]
    prod = pltpu.VMEM((2, CHUNK * PITCH, LANES), F32)
    return pl.pallas_call(
        functools.partial(power_kernel, n_dev, vregs),
        out_shape=jax.ShapeDtypeStruct((LMAX // LANES, LANES), F32),
        in_specs=[ANY] * 7,
        out_specs=VMEM,
        scratch_shapes=[pltpu.VMEM(t.shape, t.dtype) for t in [rows, u, got, *tables]]
        + [
            pltpu.VMEM((8 * (8 * vregs + 2), LANES), F32),
            prod,
            prod,
            pltpu.VMEM((2, step_blocks(n_dev) * n_dev, LANES), F32),
            pltpu.VMEM((n_dev, LANES), F32),
            pltpu.VMEM((n_dev, LANES), F32),
            pltpu.SemaphoreType.DMA((6 + PIECES,)),
        ],
        compiler_params=pltpu.CompilerParams(vmem_limit_bytes=VMEM_LIMIT),
        cost_estimate=pl.CostEstimate(flops=u.size * 4, bytes_accessed=1000000, transcendentals=0),
        name="order_power",
    )(rows, u, got, *tables)


def on_device(pixels, block_ids, block_mask, model_cl):
    n_blk = lax.axis_size("blk")
    n_mblk = lax.axis_size("mblk")
    n_dev = n_blk * n_mblk
    slots = pixels.shape[0]
    cycles = n_blk * slots // SEGS
    lats = slots * n_dev // SEGS // 2
    pairs = LMAX // (2 * n_dev)

    rows, u = legendre_rows(n_dev, lats)
    sent = cycle_spectra(pixels, block_ids, block_mask, n_dev, n_blk)
    got = lax.all_to_all(sent.reshape(n_dev, 2 * cycles, 2 * pairs), ("blk", "mblk"), 0, 0, tiled=True)
    got = got.reshape(n_dev * 2 * cycles, 2 * pairs)
    power = power_of_orders(rows, u, got, n_dev, n_blk, lats, slots)

    for axis, size in (("mblk", n_mblk), ("blk", n_blk)):
        bit = 1
        while bit < size:
            power = power + lax.ppermute(power, axis, [(i, i ^ bit) for i in range(size)])
            bit *= 2
    pseudo_cl = power.reshape(LMAX)
    rel_error = (pseudo_cl - model_cl) / model_cl
    misfit = jnp.mean(rel_error * rel_error)
    return (pseudo_cl, misfit)


def solution(mesh):
    in_specs = (P(("blk", "mblk"), None), P(("blk", "mblk")), P(("blk", "mblk")), P())
    out_specs = (P(), P())
    return jax.shard_map(
        on_device, mesh=mesh, in_specs=in_specs, out_specs=out_specs, check_vma=False
    )
```

```python
import functools
import math

import jax
import jax.numpy as jnp
import numpy as np
from jax import lax
from jax.experimental import pallas as pl
from jax.experimental.pallas import tpu as pltpu
from jax.sharding import PartitionSpec as P

NSIDE = 2048
CYCLE_PIX = 8192
LMAX = 4096
BLOCK_PIX = 1024
SEGS = 8
LANES = 128
CHUNK = 32
PITCH = 12
STREAMED = 48
PIECES = 4
VMEM_LIMIT = 56 * 1024 * 1024
POWER_VMEM = 51 * 1024 * 1024
F32 = jnp.float32
BF16 = jnp.bfloat16
ANY = pl.BlockSpec(memory_space=pl.ANY)
SMEM = pl.BlockSpec(memory_space=pltpu.SMEM)
VMEM = pl.BlockSpec(memory_space=pltpu.VMEM)


def device_index():
    return lax.axis_index("blk") * lax.axis_size("mblk") + lax.axis_index("mblk")


def split_table(table):
    high = table.astype(jnp.bfloat16)
    low = (table - high.astype(np.float64)).astype(jnp.bfloat16)
    return high, low


def split(x):
    high = x.astype(BF16)
    return high, (x - high.astype(F32)).astype(BF16)


def dot(a, b):
    return jnp.dot(a, b, preferred_element_type=F32)


def fetch(pairs, sems):
    copies = [pltpu.make_async_copy(src, dst, sems.at[i]) for i, (src, dst) in enumerate(pairs)]
    for copy in copies:
        copy.start()
    return copies


def dft_tables(n_dev):
    width = CYCLE_PIX // n_dev
    pairs = LMAX // (2 * n_dev)
    a = np.arange(n_dev)
    p2 = np.arange(n_dev)
    p1 = np.arange(width)
    one = 2.0 * np.pi * (a[:, None] * p2[None, :] % n_dev) / n_dev
    first = np.concatenate([np.cos(one), -np.sin(one), np.cos(one)[::-1], -np.sin(one)[::-1]])
    high, low = split_table(first)
    first = np.concatenate([high, low, high], axis=1)
    two = 2.0 * np.pi * a[:, None] * p1[None, :] / CYCLE_PIX
    turn = np.stack([np.cos(two), np.sin(two), np.cos(two)[::-1], np.sin(two)[::-1]])
    q = np.arange(pairs)
    second = []
    for i in (q, 2 * pairs - 1 - q):
        angle = 2.0 * np.pi * (p1[:, None] * i[None, :] % width) / width
        cos, sin = np.cos(angle), np.sin(angle)
        second.append(np.concatenate(split_table(np.block([[cos, -sin], [sin, cos]])), axis=1))
    below = a[:, None] + n_dev * q[None, :]
    half = []
    for m in (below, LMAX - 1 - below):
        angle = np.pi * m / CYCLE_PIX
        cos, sin = np.cos(angle), np.sin(angle)
        half.append(np.concatenate([cos, cos], 1))
        half.append(np.concatenate([sin, -sin], 1))
    return first, turn.astype(np.float32), np.stack(second), np.stack(half).astype(np.float32)


def dft_kernel(
    n_dev,
    n_blk,
    ids_ref,
    mask_ref,
    pix_hbm,
    first_hbm,
    turn_hbm,
    second_hbm,
    half_hbm,
    out_ref,
    x_ref,
    pix_ref,
    first_ref,
    turn_ref,
    second_ref,
    half_ref,
    sems,
):
    copies = fetch(
        [
            (pix_hbm, pix_ref),
            (first_hbm, first_ref),
            (turn_hbm, turn_ref),
            (second_hbm, second_ref),
            (half_hbm, half_ref),
        ],
        sems,
    )
    slots = pix_ref.shape[0]
    cycle_dev = slots // SEGS
    cycles = n_blk * cycle_dev
    r_band = cycle_dev * (n_dev // n_blk)
    own = lax.axis_index("mblk") * cycle_dev
    width = CYCLE_PIX // n_dev
    rows = BLOCK_PIX // width
    pairs = LMAX // (2 * n_dev)
    x_ref[...] = jnp.zeros_like(x_ref)
    copies[0].wait()
    for i in range(slots):
        number = ids_ref[i]
        cycle, seg = lax.div(number, SEGS), lax.rem(number, SEGS)
        band = lax.div(cycle, r_band)
        place = band * cycle_dev + cycle - band * r_band - own
        keep = mask_ref[i].astype(F32)
        for h in range(rows):
            x_ref[place, pl.ds(seg * rows + h, 1), :] = pix_ref[i : i + 1, h * width : (h + 1) * width] * keep
    x = jnp.concatenate([x_ref[c] for c in range(cycles)], axis=1)
    x_high, x_low = split(x)
    copies[1].wait()
    y = dot(first_ref[...], jnp.concatenate([x_high, x_high, x_low], axis=0))
    copies[2].wait()
    copies[3].wait()
    copies[4].wait()
    for phase in range(2):
        y_re = y[2 * phase * n_dev : (2 * phase + 1) * n_dev]
        y_im = y[(2 * phase + 1) * n_dev : (2 * phase + 2) * n_dev]
        cos, sin = turn_ref[2 * phase], turn_ref[2 * phase + 1]
        z = []
        for c in range(cycles):
            re, im = y_re[:, c * width : (c + 1) * width], y_im[:, c * width : (c + 1) * width]
            z.append(jnp.concatenate([re * cos + im * sin, im * cos - re * sin], axis=1))
        z_high, z_low = split(jnp.concatenate(z, axis=0))
        table = second_ref[phase]
        both = dot(z_high, table)
        spec_all = both[:, : 2 * pairs] + both[:, 2 * pairs :] + dot(z_low, table[:, : 2 * pairs])
        for c in range(cycles):
            spec = spec_all[c * n_dev : (c + 1) * n_dev]
            if c % 2 == 0:
                if 2 * pairs == LANES:
                    swapped = pltpu.roll(spec, pairs, 1)
                else:
                    swapped = jnp.concatenate([spec[:, pairs:], spec[:, :pairs]], axis=1)
                spec = spec * half_ref[2 * phase] + swapped * half_ref[2 * phase + 1]
            out_ref[pl.ds(2 * c + phase, n_dev, stride=2 * cycles), :] = spec


def cycle_spectra(pixels, block_ids, mask, n_dev, n_blk):
    pairs = LMAX // (2 * n_dev)
    cycles = n_blk * pixels.shape[0] // SEGS
    tables = [jnp.asarray(t) for t in dft_tables(n_dev)]
    return pl.pallas_call(
        functools.partial(dft_kernel, n_dev, n_blk),
        out_shape=jax.ShapeDtypeStruct((n_dev * 2 * cycles, 2 * pairs), F32),
        in_specs=[SMEM, SMEM] + [ANY] * 5,
        out_specs=VMEM,
        scratch_shapes=[pltpu.VMEM((cycles, n_dev, CYCLE_PIX // n_dev), F32), pltpu.VMEM(pixels.shape, F32)]
        + [pltpu.VMEM(t.shape, t.dtype) for t in tables]
        + [pltpu.SemaphoreType.DMA((5,))],
        compiler_params=pltpu.CompilerParams(vmem_limit_bytes=VMEM_LIMIT),
        name="cycle_dft",
    )(block_ids, mask, pixels, *tables)


def wallis(count):
    value = np.zeros(count)
    k = np.arange(0, count - 2, 2)
    value[0::2] = np.concatenate([[1.0], np.cumprod((k + 1.0) / (k + 2.0))])[: len(value[0::2])]
    value[1::2] = 2.0 / np.pi * np.concatenate([[1.0], np.cumprod((k + 2.0) / (k + 3.0))])[: len(value[1::2])]
    return value


def step_blocks(n_dev):
    blocks = LMAX // n_dev + 1
    return blocks + blocks * (n_dev // CHUNK) % 2


def latitude_lanes(n_dev, lats):
    pairs = LMAX // (2 * n_dev)
    x = (lats - np.arange(lats)) * (2.0 / (3.0 * NSIDE))
    reps = LANES // pairs
    order = np.arange(lats).reshape(-1, reps, 8)
    return np.repeat(x[order].transpose(0, 2, 1), pairs, axis=2).reshape(-1, LANES)


def recurrence_tables(n_dev, lats):
    pairs = LMAX // (2 * n_dev)
    total = step_blocks(n_dev) * n_dev
    value = wallis(2 * LMAX + 6 * n_dev + total)
    tau = np.arange(total)[:, None]
    q = np.arange(pairs)[None, :]
    rise = np.where(q < tau // n_dev, tau - n_dev * (q + 1), tau)
    wide = np.arange(total + 2 * n_dev)[:, None]
    t_low = value[np.maximum(wide - n_dev + n_dev * q, 0)]
    t_high = value[wide + 2 * LMAX - 2 - 2 * n_dev * q - 2 * (n_dev - 1)]
    x = latitude_lanes(n_dev, lats)
    x_tabs = np.stack([x, x * x, 0.5 * np.log1p(-x * x)])
    tables = [np.tile(t, (1, LANES // pairs)) for t in (value[rise], t_low, t_high)]
    return [t.astype(np.float32) for t in tables + [x_tabs]]


def advance(coef_ref, row, even, odd, x2):
    one, two = coef_ref[pl.ds(row, 1), :], coef_ref[pl.ds(row + 1, 1), :]
    fresh_odd = [one * e - o for e, o in zip(even, odd)]
    gains = [two * x for x in x2]
    fresh_even = [(g * one - 1.0) * e - g * o for g, e, o in zip(gains, even, odd)]
    return fresh_even, fresh_odd


def turn_lanes(chunk, per_block, q, seeds, even, odd):
    turned = q == lax.div(chunk, per_block) - 1
    if per_block > 1:
        turned = jnp.logical_and(turned, lax.rem(chunk, per_block) == 0)
    return [jnp.where(turned, s, e) for s, e in zip(seeds, even)], [jnp.where(turned, 0.0, o) for o in odd]


def recurrence_kernel(
    n_dev,
    vregs,
    pixel_total,
    rise_hbm,
    low_hbm,
    high_hbm,
    x_hbm,
    rows_hbm,
    u_hbm,
    rise_ref,
    low_ref,
    high_ref,
    x_ref,
    rows_ref,
    u_ref,
    sems,
):
    pairs = LMAX // (2 * n_dev)
    per_block = n_dev // CHUNK
    chunks = step_blocks(n_dev) * per_block
    total = chunks * CHUNK
    cut = STREAMED * CHUNK
    parts = [(x_hbm, x_ref)]
    for start, stop in ((0, cut), (cut, total)):
        for src, dst in ((rise_hbm, rise_ref), (low_hbm, low_ref), (high_hbm, high_ref)):
            reach = 0 if src is rise_hbm else 2 * n_dev
            first = start + reach if start else 0
            span = pl.ds(first, stop + reach - first)
            parts.append((src.at[span], dst.at[span]))
    copies = fetch(parts, sems)
    d = device_index()
    lane = lax.broadcasted_iota(jnp.int32, (8, LANES), 1)
    sub = lax.broadcasted_iota(jnp.int32, (8, LANES), 0)
    q = lax.rem(lane, pairs)
    m_low = (d + n_dev * q).astype(F32)
    m_high = (LMAX - 1.0) - m_low
    weight_low = jnp.where(m_low == 0.0, 1.0, 2.0) / pixel_total
    weight_high = jnp.full((8, LANES), 2.0 / pixel_total, F32)
    l_low = sub.astype(F32) + (d.astype(F32) - n_dev)
    l_high = sub.astype(F32) + m_high
    for copy in copies[:4]:
        copy.wait()
    x2 = [x_ref[1, 8 * v : 8 * v + 8, :] for v in range(vregs)]
    logs = [x_ref[2, 8 * v : 8 * v + 8, :] for v in range(vregs)]
    seed_low = [jnp.exp(m_low * g) for g in logs]
    seed_high = [jnp.exp(m_high * g) for g in logs]

    def coefficients(start, stop):
        many = max(n for n in range(1, 13) if (stop - start) % n == 0)

        def some(group, carry):
            fresh = []
            for step in range(many):
                chunk = start + group * many + step
                is_low = q < lax.div(chunk, per_block)
                weight = jnp.where(is_low, weight_low, weight_high)
                first = jnp.where(is_low, l_low, l_high) + (chunk * CHUNK).astype(F32)
                for i in range(CHUNK // 8):
                    tau = pl.multiple_of(chunk * CHUNK, CHUNK) + 8 * i
                    low = low_ref[pl.ds(tau + 2 * d, 8), :]
                    high = high_ref[pl.ds(tau + 2 * (n_dev - 1 - d), 8), :]
                    product = rise_ref[pl.ds(tau, 8), :] * jnp.where(is_low, low, high)
                    degree = first + 8.0 * i
                    coef = product * (degree * math.pi + 0.5 * math.pi)
                    fresh.append((tau, coef, jnp.where(degree < LMAX, product * weight, 0.0)))
            for tau, coef, weight in fresh:
                rows_ref[pl.ds(tau, 8), :] = coef
                rows_ref[pl.ds(total + tau, 8), :] = weight
            return carry

        lax.fori_loop(0, (stop - start) // many, some, 0)

    def steps(chunk, state):
        even, odd = turn_lanes(chunk, per_block, q, seed_low, list(state[:vregs]), list(state[vregs:]))
        first = pl.multiple_of(chunk * CHUNK, CHUNK)
        start = pl.multiple_of(chunk * (CHUNK * 8 * vregs), CHUNK * 8 * vregs)
        for s in range(0, CHUNK, 2):
            fresh_even, fresh_odd = advance(rows_ref, first + s, even, odd, x2)
            for v in range(vregs):
                u_ref[pl.ds(start + 8 * (s * vregs + v), 8), :] = even[v]
                u_ref[pl.ds(start + 8 * ((s + 1) * vregs + v), 8), :] = fresh_odd[v]
            even, odd = fresh_even, fresh_odd
        return (*even, *odd)

    coefficients(0, STREAMED)
    zero = jnp.zeros((8, LANES), F32)
    state = (*seed_high, *([zero] * vregs))
    piece = STREAMED // PIECES
    size = piece * CHUNK * 8 * vregs
    out = []

    def send(src, dst, sem):
        out.append(pltpu.make_async_copy(src, dst, sems.at[sem]))
        out[-1].start()

    for p in range(PIECES):
        first = p * piece
        state = lax.fori_loop(first // 2, (first + piece) // 2, lambda h, s: steps(2 * h + 1, steps(2 * h, s)), state)
        extra = 0
        if p == PIECES - 1:
            extra = 16 * vregs
            for v in range(2 * vregs):
                u_ref[PIECES * size + 8 * v : PIECES * size + 8 * v + 8, :] = state[v]
        span = pl.ds(p * size, size + extra)
        send(u_ref.at[span], u_hbm.at[span], 7 + p)
    for copy in copies[4:]:
        copy.wait()
    coefficients(STREAMED, chunks)
    send(rows_ref.at[pl.ds(cut, 2 * total - cut)], rows_hbm, 7 + PIECES)
    for copy in out:
        copy.wait()


def legendre_rows(n_dev, lats):
    pairs = LMAX // (2 * n_dev)
    vregs = lats * pairs // (8 * LANES)
    total = step_blocks(n_dev) * n_dev
    cut = STREAMED * CHUNK
    tables = [jnp.asarray(t) for t in recurrence_tables(n_dev, lats)]
    rows = jax.ShapeDtypeStruct((2 * total, LANES), F32)
    rest = jax.ShapeDtypeStruct((2 * total - cut, LANES), F32)
    u = jax.ShapeDtypeStruct((cut * 8 * vregs + 16 * vregs, LANES), F32)
    return pl.pallas_call(
        functools.partial(recurrence_kernel, n_dev, vregs, float(2 * lats * CYCLE_PIX)),
        out_shape=(rest, u),
        in_specs=[ANY] * 4,
        out_specs=(ANY, ANY),
        scratch_shapes=[pltpu.VMEM(t.shape, t.dtype) for t in [*tables, rows, u]]
        + [pltpu.SemaphoreType.DMA((8 + PIECES,))],
        compiler_params=pltpu.CompilerParams(vmem_limit_bytes=VMEM_LIMIT),
        cost_estimate=pl.CostEstimate(flops=total * 8 * LANES * vregs * 8, bytes_accessed=25000000, transcendentals=0),
        name="legendre_rows",
    )(*tables)


def power_tables(n_dev, n_blk, lats, slots):
    pairs = LMAX // (2 * n_dev)
    cycles_all = 2 * lats
    n_mblk = n_dev // n_blk
    cycle_dev = slots // SEGS
    r_band = cycle_dev * n_mblk
    col = 2 * n_blk * cycle_dev
    pick = np.zeros((4 * lats + 16, n_dev * col))

    def put(row, cycle, phase, weight):
        band, inner = divmod(cycle, r_band)
        j, k = divmod(inner, cycle_dev)
        for s in range(n_blk):
            pick[row, (s * n_mblk + j) * col + (band * cycle_dev + k) * 2 + phase] += weight

    for phase in range(2):
        for n in range(lats):
            for odd in range(2):
                row = (2 * phase + odd) * lats + n
                put(row, n, phase, 1.0)
                if n:
                    put(row, cycles_all - n, phase, -1.0 if odd else 1.0)
        put(4 * lats + phase, lats, phase, 1.0)

    lane = np.arange(LANES)
    band_of = (3 * pairs - 2 - lane) % LANES
    copies = LANES // n_dev
    spread = (band_of[None, :] % copies == (lane // n_dev)[:, None]) & (band_of[None, :] < 2 * pairs)
    gather = band_of[None, :] // copies == np.arange(LMAX // LANES)[:, None]
    return (
        pick.astype(jnp.bfloat16),
        recurrence_tables(n_dev, lats)[3],
        spread.astype(np.float32),
        gather.astype(jnp.bfloat16),
    )


def exact_dot(zero_one, x, dims):
    total = None
    for _ in range(3):
        part = x.astype(BF16)
        x = x - part.astype(F32)
        term = lax.dot_general(zero_one, part, (dims, ((), ())), preferred_element_type=F32)
        total = term if total is None else total + term
    return total


def power_kernel(
    n_dev,
    vregs,
    rows_hbm,
    u_hbm,
    got_ref,
    pick_ref,
    x_ref,
    spread_ref,
    gather_ref,
    out_ref,
    rows_ref,
    u_ref,
    f_ref,
    prod_a,
    prod_b,
    sum_ref,
    accl_ref,
    acch_ref,
    sems,
):
    pairs = LMAX // (2 * n_dev)
    all_steps = step_blocks(n_dev) * n_dev
    cut = STREAMED * CHUNK
    size = cut // PIECES * 8 * vregs
    spans = [pl.ds(p * size, size) for p in range(PIECES)]
    states, coefs, weights = pl.ds(PIECES * size, 16 * vregs), pl.ds(0, all_steps - cut), pl.ds(all_steps - cut, all_steps)
    copies = fetch(
        [
            (u_hbm.at[states], u_ref.at[states]),
            (rows_hbm.at[coefs], rows_ref.at[coefs]),
        ],
        sems,
    )
    d = device_index()
    reps = LANES // pairs
    lats = vregs * 8 * reps
    per_block = n_dev // CHUNK
    blocks = step_blocks(n_dev)
    chunks = blocks * per_block
    lane = lax.broadcasted_iota(jnp.int32, (8, LANES), 1)
    sub = lax.broadcasted_iota(jnp.int32, (8, LANES), 0)
    q = lax.rem(lane, pairs)
    head = lane < pairs
    sign = jnp.where(sub % 4 == 0, 1.0, jnp.where(sub % 4 == 2, -1.0, 0.0)).astype(F32)
    accl_ref[...] = jnp.zeros_like(accl_ref)
    acch_ref[...] = jnp.zeros_like(acch_ref)
    prod_b[...] = jnp.zeros_like(prod_b)

    f_all = exact_dot(pick_ref[...], got_ref[...], ((1,), (0,)))

    def store(slot, value):
        f_ref[8 * slot : 8 * slot + 8, :] = value

    def load(slot):
        return f_ref[8 * slot : 8 * slot + 8, :]

    for phase in range(2):
        for odd in range(2):
            for v in range(vregs):
                for part in range(2):
                    pieces = []
                    for h in range(reps):
                        row = (2 * phase + odd) * lats + (v * reps + h) * 8
                        pieces.append(f_all[row : row + 8, part * pairs : (part + 1) * pairs])
                    value = jnp.concatenate(pieces, axis=1)
                    if odd:
                        value = value * x_ref[0, 8 * v : 8 * v + 8, :]
                    store(((phase * 2 + odd) * vregs + v) * 2 + part, value)
    base = 8 * vregs
    for phase in range(2):
        row = f_all[4 * lats + phase : 4 * lats + phase + 1, :]
        if 2 * pairs < LANES:
            row = jnp.concatenate([row, jnp.zeros((1, LANES - 2 * pairs), F32)], axis=1)
        store(base + phase, jnp.broadcast_to(row, (8, LANES)) * sign)

    def spectra_now(chunk):
        is_low = q < lax.div(chunk, per_block)

        def now(o, v, p):
            return jnp.where(is_low, load((o * vregs + v) * 2 + p), load(((2 + o) * vregs + v) * 2 + p))

        return [[[now(o, v, p) for p in range(2)] for v in range(vregs)] for o in range(2)]

    def product(s, u, now, prod_ref):
        for part in range(2):
            value = u[0] * now[s % 2][0][part]
            for v in range(1, vregs):
                value = value + u[v] * now[s % 2][v][part]
            prod_ref[part, pl.ds((s // 8) * 8 * PITCH + s % 8, 8, stride=PITCH), :] = value

    def products(chunk, prod_ref):
        now = spectra_now(chunk)
        start = pl.multiple_of(chunk * (CHUNK * 8 * vregs), CHUNK * 8 * vregs)
        for s in range(CHUNK):
            product(s, [u_ref[pl.ds(start + 8 * (s * vregs + v), 8), :] for v in range(vregs)], now, prod_ref)

    def steps(chunk, prod_ref, state):
        now = spectra_now(chunk)
        even, odd = turn_lanes(chunk, per_block, q, seed_low, list(state[:vregs]), list(state[vregs:]))
        first = pl.multiple_of((chunk - STREAMED) * CHUNK, CHUNK)
        for s in range(0, CHUNK, 2):
            fresh_even, fresh_odd = advance(rows_ref, first + s, even, odd, x2)
            product(s, even, now, prod_ref)
            product(s + 1, fresh_odd, now, prod_ref)
            even, odd = fresh_even, fresh_odd
        return (*even, *odd)

    def reduce(chunk, prod_ref):
        for i in range(CHUNK // 8):
            for part in range(2):
                rows = [prod_ref[part, pl.ds((8 * i + s) * PITCH, 8), :] for s in range(8)]
                while len(rows) > 1:
                    rows = [a + b for a, b in zip(rows[::2], rows[1::2])]
                sum_ref[part, pl.ds(pl.multiple_of(chunk * CHUNK, CHUNK) + 8 * i, 8), :] = rows[0]

    def two_inline(h, state):
        state = steps(2 * h, prod_a, state)
        reduce(jnp.maximum(2 * h - 1, STREAMED), prod_b)
        state = steps(2 * h + 1, prod_b, state)
        reduce(2 * h, prod_a)
        return state

    def two_streamed(h, carry):
        products(2 * h, prod_a)
        reduce(jnp.maximum(2 * h - 1, 0), prod_b)
        products(2 * h + 1, prod_b)
        reduce(2 * h, prod_a)
        return carry

    m_low = (d + n_dev * q).astype(F32)
    x2 = [x_ref[1, 8 * v : 8 * v + 8, :] for v in range(vregs)]
    seed_low = [jnp.exp(m_low * x_ref[2, 8 * v : 8 * v + 8, :]) for v in range(vregs)]
    for copy in copies:
        copy.wait()
    moved = [(u_hbm.at[span], u_ref.at[span]) for span in spans] + [
        (rows_hbm.at[weights], rows_ref.at[weights]),
    ]
    copies = [pltpu.make_async_copy(src, dst, sems.at[2 + i]) for i, (src, dst) in enumerate(moved)]
    for copy in copies:
        copy.start()
    state = [u_ref[PIECES * size + 8 * v : PIECES * size + 8 * v + 8, :] for v in range(2 * vregs)]
    lax.fori_loop(STREAMED // 2, chunks // 2, two_inline, tuple(state))
    reduce(chunks - 1, prod_b)
    piece = STREAMED // PIECES
    for p in range(PIECES):
        copies[p].wait()
        lax.fori_loop(p * piece // 2, (p + 1) * piece // 2, two_streamed, 0)
    reduce(STREAMED - 1, prod_b)
    for copy in copies[PIECES:]:
        copy.wait()

    def packed(tau):
        re, im = sum_ref[0, pl.ds(tau, 8), :], sum_ref[1, pl.ds(tau, 8), :]
        if 2 * pairs == LANES:
            return jnp.where(head, re, im) + pltpu.roll(jnp.where(head, im, re), pairs, 1)
        step = pairs
        while step < LANES:
            re, im = re + pltpu.roll(re, step, 1), im + pltpu.roll(im, step, 1)
            step *= 2
        return jnp.where(head, re, jnp.where(lane < 2 * pairs, im, 0.0))

    def powers(first, count, with_high):
        tiles = n_dev // 8
        places = [(i, j) for j in range(count) for i in range(tiles)]
        taus = [pl.multiple_of((first + j) * n_dev, n_dev) + 8 * i for i, j in places]
        lows = [q < first + j for j in range(count)]
        flats = [load(base)] * count
        if with_high:
            flats = [jnp.where(low, load(base), load(base + 1)) for low in lows]
        values = [packed(tau) for tau in taus]
        values = [v + flats[j] for v, (_, j) in zip(values, places)]
        values = [v * v * rows_ref[pl.ds(all_steps - cut + tau, 8), :] for v, tau in zip(values, taus)]
        low_parts = values
        if with_high:
            low_parts = [jnp.where(lows[j], v, 0.0) for v, (_, j) in zip(values, places)]
            high_parts = [v - low for v, low in zip(values, low_parts)]
        sums = [jnp.sum(v, axis=1, keepdims=True) for v in low_parts]
        if with_high:
            shifts = [count - 1 - j for _, j in places]
            high_parts = [pltpu.roll(v, shift, 1) if shift else v for v, shift in zip(high_parts, shifts)]
        for i in range(tiles):
            total = accl_ref[8 * i : 8 * i + 8, :]
            for j in range(count):
                target = lax.rem(3 * pairs - 1 - (first + j) + 2 * LANES, LANES)
                total = total + jnp.where(lane == target, sums[j * tiles + i], 0.0)
            accl_ref[8 * i : 8 * i + 8, :] = total
            if with_high:
                total = pltpu.roll(acch_ref[8 * i : 8 * i + 8, :], count, 1)
                for j in range(count):
                    total = total + high_parts[j * tiles + i]
                acch_ref[8 * i : 8 * i + 8, :] = total

    many = 512 // n_dev
    half = pairs // many

    def both_halves(g, carry):
        powers(g * many, many, True)
        return carry

    def low_half(g, carry):
        powers(g * many, many, False)
        return carry

    lax.fori_loop(0, half, both_halves, 0)
    lax.fori_loop(half, blocks // many, low_half, 0)
    if blocks % many:
        powers(jnp.int32(blocks - blocks % many), blocks % many, False)

    rows = lax.broadcasted_iota(jnp.int32, (n_dev, LANES), 0)

    def shifted(acc, shift):
        rolled = pltpu.roll(acc, shift, 0)
        return jnp.where(rows < shift, pltpu.roll(rolled, LANES - 1, 1), rolled)

    lanes = lax.broadcasted_iota(jnp.int32, (n_dev, LANES), 1)
    high = acch_ref[...] + pltpu.roll(acch_ref[...], LANES - pairs, 1)
    high = jnp.where(jnp.logical_and(lanes >= pairs - 1, lanes < 2 * pairs - 1), high, 0.0)
    power = shifted(accl_ref[...], d) + shifted(high, n_dev - 1 - d)
    tall = jnp.concatenate([power] * (LANES // n_dev), axis=0) * spread_ref[...]
    out_ref[...] = exact_dot(gather_ref[...], tall, ((1,), (1,)))


def power_of_orders(rows, u, got, n_dev, n_blk, lats, slots):
    pairs = LMAX // (2 * n_dev)
    vregs = lats * pairs // (8 * LANES)
    tables = [jnp.asarray(t) for t in power_tables(n_dev, n_blk, lats, slots)]
    prod = pltpu.VMEM((2, CHUNK * PITCH, LANES), F32)
    return pl.pallas_call(
        functools.partial(power_kernel, n_dev, vregs),
        out_shape=jax.ShapeDtypeStruct((LMAX // LANES, LANES), F32),
        in_specs=[ANY] * 2 + [VMEM] * 5,
        out_specs=VMEM,
        scratch_shapes=[pltpu.VMEM(t.shape, t.dtype) for t in [rows, u]]
        + [
            pltpu.VMEM((8 * (8 * vregs + 2), LANES), F32),
            prod,
            prod,
            pltpu.VMEM((2, step_blocks(n_dev) * n_dev, LANES), F32),
            pltpu.VMEM((n_dev, LANES), F32),
            pltpu.VMEM((n_dev, LANES), F32),
            pltpu.SemaphoreType.DMA((3 + PIECES,)),
        ],
        compiler_params=pltpu.CompilerParams(vmem_limit_bytes=POWER_VMEM),
        cost_estimate=pl.CostEstimate(flops=u.size * 4, bytes_accessed=1000000, transcendentals=0),
        name="order_power",
    )(rows, u, got, *tables)


def on_device(pixels, block_ids, block_mask, model_cl):
    n_blk = lax.axis_size("blk")
    n_mblk = lax.axis_size("mblk")
    n_dev = n_blk * n_mblk
    slots = pixels.shape[0]
    cycles = n_blk * slots // SEGS
    lats = slots * n_dev // SEGS // 2
    pairs = LMAX // (2 * n_dev)

    rows, u = legendre_rows(n_dev, lats)
    sent = cycle_spectra(pixels, block_ids, block_mask, n_dev, n_blk)
    got = lax.all_to_all(sent.reshape(n_dev, 2 * cycles, 2 * pairs), ("blk", "mblk"), 0, 0, tiled=True)
    got = got.reshape(n_dev * 2 * cycles, 2 * pairs)
    power = power_of_orders(rows, u, got, n_dev, n_blk, lats, slots)

    for axis, size in (("mblk", n_mblk), ("blk", n_blk)):
        bit = 1
        while bit < size:
            power = power + lax.ppermute(power, axis, [(i, i ^ bit) for i in range(size)])
            bit *= 2
    pseudo_cl = power.reshape(LMAX)
    rel_error = (pseudo_cl - model_cl) / model_cl
    misfit = jnp.mean(rel_error * rel_error)
    return (pseudo_cl, misfit)


def solution(mesh):
    in_specs = (P(("blk", "mblk"), None), P(("blk", "mblk")), P(("blk", "mblk")), P())
    out_specs = (P(), P())
    return jax.shard_map(
        on_device, mesh=mesh, in_specs=in_specs, out_specs=out_specs, check_vma=False
    )
```

```python
import functools
import math

import jax
import jax.numpy as jnp
import numpy as np
from jax import lax
from jax.experimental import pallas as pl
from jax.experimental.pallas import tpu as pltpu
from jax.sharding import PartitionSpec as P

NSIDE = 2048
CYCLE_PIX = 8192
LMAX = 4096
BLOCK_PIX = 1024
SEGS = 8
LANES = 128
CHUNK = 32
PITCH = 12
STREAMED = 96
PIECES = 6
VMEM_LIMIT = 56 * 1024 * 1024
POWER_VMEM = 51 * 1024 * 1024
F32 = jnp.float32
BF16 = jnp.bfloat16
ANY = pl.BlockSpec(memory_space=pl.ANY)
VMEM = pl.BlockSpec(memory_space=pltpu.VMEM)


def device_index():
    return lax.axis_index("blk") * lax.axis_size("mblk") + lax.axis_index("mblk")


def split_table(table):
    high = table.astype(jnp.bfloat16)
    low = (table - high.astype(np.float64)).astype(jnp.bfloat16)
    return high, low


def split(x):
    high = x.astype(BF16)
    return high, (x - high.astype(F32)).astype(BF16)


def dot(a, b):
    return jnp.dot(a, b, preferred_element_type=F32)


def fetch(pairs, sems):
    copies = [pltpu.make_async_copy(src, dst, sems.at[i]) for i, (src, dst) in enumerate(pairs)]
    for copy in copies:
        copy.start()
    return copies


def dft_tables(n_dev):
    width = CYCLE_PIX // n_dev
    pairs = LMAX // (2 * n_dev)
    a = np.arange(n_dev)
    p2 = np.arange(n_dev)
    p1 = np.arange(width)
    one = 2.0 * np.pi * (a[:, None] * p2[None, :] % n_dev) / n_dev
    first = np.concatenate([np.cos(one), -np.sin(one), np.cos(one)[::-1], -np.sin(one)[::-1]])
    high, low = split_table(first)
    first = np.concatenate([high, low, high], axis=1)
    two = 2.0 * np.pi * a[:, None] * p1[None, :] / CYCLE_PIX
    turn = np.stack([np.cos(two), np.sin(two), np.cos(two)[::-1], np.sin(two)[::-1]])
    q = np.arange(pairs)
    second = []
    for i in (q, 2 * pairs - 1 - q):
        angle = 2.0 * np.pi * (p1[:, None] * i[None, :] % width) / width
        cos, sin = np.cos(angle), np.sin(angle)
        second.append(np.concatenate(split_table(np.block([[cos, -sin], [sin, cos]])), axis=1))
    below = a[:, None] + n_dev * q[None, :]
    half = []
    for m in (below, LMAX - 1 - below):
        angle = np.pi * m / CYCLE_PIX
        cos, sin = np.cos(angle), np.sin(angle)
        half.append(np.concatenate([cos, cos], 1))
        half.append(np.concatenate([sin, -sin], 1))
    return first, turn.astype(np.float32), np.stack(second), np.stack(half).astype(np.float32)


def dft_kernel(
    n_dev,
    n_blk,
    ids_hbm,
    mask_hbm,
    pix_hbm,
    first_hbm,
    turn_hbm,
    second_hbm,
    half_hbm,
    out_hbm,
    out_ref,
    x_ref,
    ids_ref,
    mask_ref,
    pix_ref,
    first_ref,
    turn_ref,
    second_ref,
    half_ref,
    sems,
):
    copies = fetch(
        [
            (ids_hbm, ids_ref),
            (mask_hbm, mask_ref),
            (pix_hbm, pix_ref),
            (first_hbm, first_ref),
            (turn_hbm, turn_ref),
            (second_hbm, second_ref),
            (half_hbm, half_ref),
        ],
        sems,
    )
    slots = pix_ref.shape[0]
    cycle_dev = slots // SEGS
    cycles = n_blk * cycle_dev
    r_band = cycle_dev * (n_dev // n_blk)
    own = lax.axis_index("mblk") * cycle_dev
    width = CYCLE_PIX // n_dev
    rows = BLOCK_PIX // width
    pairs = LMAX // (2 * n_dev)
    x_ref[...] = jnp.zeros_like(x_ref)
    for copy in copies[:3]:
        copy.wait()
    for i in range(slots):
        number = ids_ref[i]
        cycle, seg = lax.div(number, SEGS), lax.rem(number, SEGS)
        band = lax.div(cycle, r_band)
        place = band * cycle_dev + cycle - band * r_band - own
        keep = mask_ref[i].astype(F32)
        for h in range(rows):
            x_ref[place, pl.ds(seg * rows + h, 1), :] = pix_ref[i : i + 1, h * width : (h + 1) * width] * keep
    x = jnp.concatenate([x_ref[c] for c in range(cycles)], axis=1)
    x_high, x_low = split(x)
    copies[3].wait()
    y = dot(first_ref[...], jnp.concatenate([x_high, x_high, x_low], axis=0))
    for copy in copies[4:]:
        copy.wait()
    for phase in range(2):
        y_re = y[2 * phase * n_dev : (2 * phase + 1) * n_dev]
        y_im = y[(2 * phase + 1) * n_dev : (2 * phase + 2) * n_dev]
        cos, sin = turn_ref[2 * phase], turn_ref[2 * phase + 1]
        z = []
        for c in range(cycles):
            re, im = y_re[:, c * width : (c + 1) * width], y_im[:, c * width : (c + 1) * width]
            z.append(jnp.concatenate([re * cos + im * sin, im * cos - re * sin], axis=1))
        z_high, z_low = split(jnp.concatenate(z, axis=0))
        table = second_ref[phase]
        both = dot(z_high, table)
        spec_all = both[:, : 2 * pairs] + both[:, 2 * pairs :] + dot(z_low, table[:, : 2 * pairs])
        for c in range(cycles):
            spec = spec_all[c * n_dev : (c + 1) * n_dev]
            if c % 2 == 0:
                if 2 * pairs == LANES:
                    swapped = pltpu.roll(spec, pairs, 1)
                else:
                    swapped = jnp.concatenate([spec[:, pairs:], spec[:, :pairs]], axis=1)
                spec = spec * half_ref[2 * phase] + swapped * half_ref[2 * phase + 1]
            out_ref[pl.ds(2 * c + phase, n_dev, stride=2 * cycles), :] = spec
    send = pltpu.make_async_copy(out_ref, out_hbm, sems.at[7])
    send.start()
    send.wait()


def cycle_spectra(pixels, block_ids, mask, n_dev, n_blk):
    pairs = LMAX // (2 * n_dev)
    cycles = n_blk * pixels.shape[0] // SEGS
    tables = [jnp.asarray(t) for t in dft_tables(n_dev)]
    out = jax.ShapeDtypeStruct((n_dev * 2 * cycles, 2 * pairs), F32)
    return pl.pallas_call(
        functools.partial(dft_kernel, n_dev, n_blk),
        out_shape=out,
        in_specs=[ANY] * 7,
        out_specs=ANY,
        scratch_shapes=[pltpu.VMEM(out.shape, F32), pltpu.VMEM((cycles, n_dev, CYCLE_PIX // n_dev), F32)]
        + [pltpu.SMEM(block_ids.shape, jnp.int32), pltpu.SMEM(mask.shape, jnp.int32)]
        + [pltpu.VMEM(t.shape, t.dtype) for t in [pixels, *tables]]
        + [pltpu.SemaphoreType.DMA((8,))],
        compiler_params=pltpu.CompilerParams(vmem_limit_bytes=VMEM_LIMIT),
        name="cycle_dft",
    )(block_ids, mask, pixels, *tables)


def wallis(count):
    value = np.zeros(count)
    k = np.arange(0, count - 2, 2)
    value[0::2] = np.concatenate([[1.0], np.cumprod((k + 1.0) / (k + 2.0))])[: len(value[0::2])]
    value[1::2] = 2.0 / np.pi * np.concatenate([[1.0], np.cumprod((k + 2.0) / (k + 3.0))])[: len(value[1::2])]
    return value


def step_blocks(n_dev):
    blocks = LMAX // n_dev + 1
    return blocks + blocks * (n_dev // CHUNK) % 2


def latitude_lanes(n_dev, lats):
    pairs = LMAX // (2 * n_dev)
    x = (lats - np.arange(lats)) * (2.0 / (3.0 * NSIDE))
    reps = LANES // pairs
    order = np.arange(lats).reshape(-1, reps, 8)
    return np.repeat(x[order].transpose(0, 2, 1), pairs, axis=2).reshape(-1, LANES)


def recurrence_tables(n_dev, lats):
    pairs = LMAX // (2 * n_dev)
    total = step_blocks(n_dev) * n_dev
    value = wallis(2 * LMAX + 6 * n_dev + total)
    tau = np.arange(total)[:, None]
    q = np.arange(pairs)[None, :]
    rise = np.where(q < tau // n_dev, tau - n_dev * (q + 1), tau)
    wide = np.arange(total + 2 * n_dev)[:, None]
    t_low = value[np.maximum(wide - n_dev + n_dev * q, 0)]
    t_high = value[wide + 2 * LMAX - 2 - 2 * n_dev * q - 2 * (n_dev - 1)]
    x = latitude_lanes(n_dev, lats)
    x_tabs = np.stack([x, x * x, 0.5 * np.log1p(-x * x)])
    tables = [np.tile(t, (1, LANES // pairs)) for t in (value[rise], t_low, t_high)]
    return [t.astype(np.float32) for t in tables + [x_tabs]]


def advance(coef_ref, row, even, odd, x2):
    one, two = coef_ref[pl.ds(row, 1), :], coef_ref[pl.ds(row + 1, 1), :]
    fresh_odd = [one * e - o for e, o in zip(even, odd)]
    gains = [two * x for x in x2]
    fresh_even = [(g * one - 1.0) * e - g * o for g, e, o in zip(gains, even, odd)]
    return fresh_even, fresh_odd


def turn_lanes(chunk, per_block, q, seeds, even, odd):
    turned = q == lax.div(chunk, per_block) - 1
    if per_block > 1:
        turned = jnp.logical_and(turned, lax.rem(chunk, per_block) == 0)
    return [jnp.where(turned, s, e) for s, e in zip(seeds, even)], [jnp.where(turned, 0.0, o) for o in odd]


def recurrence_kernel(
    n_dev,
    vregs,
    pixel_total,
    rise_hbm,
    low_hbm,
    high_hbm,
    x_hbm,
    rows_hbm,
    u_hbm,
    rise_ref,
    low_ref,
    high_ref,
    x_ref,
    rows_ref,
    u_ref,
    sems,
):
    pairs = LMAX // (2 * n_dev)
    per_block = n_dev // CHUNK
    chunks = step_blocks(n_dev) * per_block
    total = chunks * CHUNK
    piece = STREAMED // PIECES
    ends = [0, 2 * piece * CHUNK, STREAMED * CHUNK, total]
    parts = [(x_hbm, x_ref)]
    for start, stop in zip(ends, ends[1:]):
        for src, dst in ((rise_hbm, rise_ref), (low_hbm, low_ref), (high_hbm, high_ref)):
            reach = 0 if src is rise_hbm else 2 * n_dev
            first = start + reach if start else 0
            span = pl.ds(first, stop + reach - first)
            parts.append((src.at[span], dst.at[span]))
    copies = fetch(parts, sems)
    d = device_index()
    lane = lax.broadcasted_iota(jnp.int32, (8, LANES), 1)
    sub = lax.broadcasted_iota(jnp.int32, (8, LANES), 0)
    q = lax.rem(lane, pairs)
    m_low = (d + n_dev * q).astype(F32)
    m_high = (LMAX - 1.0) - m_low
    weight_low = jnp.where(m_low == 0.0, 1.0, 2.0) / pixel_total
    weight_high = jnp.full((8, LANES), 2.0 / pixel_total, F32)
    l_low = sub.astype(F32) + (d.astype(F32) - n_dev)
    l_high = sub.astype(F32) + m_high
    for copy in copies[:4]:
        copy.wait()
    x2 = [x_ref[1, 8 * v : 8 * v + 8, :] for v in range(vregs)]
    logs = [x_ref[2, 8 * v : 8 * v + 8, :] for v in range(vregs)]
    seed_low = [jnp.exp(m_low * g) for g in logs]
    seed_high = [jnp.exp(m_high * g) for g in logs]

    def coefficients(start, stop):
        many = max(n for n in range(1, 13) if (stop - start) % n == 0)

        def some(group, carry):
            fresh = []
            for step in range(many):
                chunk = start + group * many + step
                is_low = q < lax.div(chunk, per_block)
                weight = jnp.where(is_low, weight_low, weight_high)
                first = jnp.where(is_low, l_low, l_high) + (chunk * CHUNK).astype(F32)
                for i in range(CHUNK // 8):
                    tau = pl.multiple_of(chunk * CHUNK, CHUNK) + 8 * i
                    low = low_ref[pl.ds(tau + 2 * d, 8), :]
                    high = high_ref[pl.ds(tau + 2 * (n_dev - 1 - d), 8), :]
                    product = rise_ref[pl.ds(tau, 8), :] * jnp.where(is_low, low, high)
                    degree = first + 8.0 * i
                    coef = product * (degree * math.pi + 0.5 * math.pi)
                    fresh.append((tau, coef, jnp.where(degree < LMAX, product * weight, 0.0)))
            for tau, coef, weight in fresh:
                rows_ref[pl.ds(tau, 8), :] = coef
                rows_ref[pl.ds(total + tau, 8), :] = weight
            return carry

        lax.fori_loop(0, (stop - start) // many, some, 0)

    def steps(chunk, state):
        even, odd = turn_lanes(chunk, per_block, q, seed_low, list(state[:vregs]), list(state[vregs:]))
        first = pl.multiple_of(chunk * CHUNK, CHUNK)
        start = pl.multiple_of(chunk * (CHUNK * 4 * vregs), CHUNK * 4 * vregs)
        for s in range(0, CHUNK, 2):
            fresh_even, fresh_odd = advance(rows_ref, first + s, even, odd, x2)
            for v in range(vregs):
                u_ref[pl.ds(start + 8 * (s // 2 * vregs + v), 8), :] = even[v]
            even, odd = fresh_even, fresh_odd
        return (*even, *odd)

    zero = jnp.zeros((8, LANES), F32)
    state = (*seed_high, *([zero] * vregs))
    size = piece * CHUNK * 4 * vregs
    out = []

    def send(src, dst, sem):
        out.append(pltpu.make_async_copy(src, dst, sems.at[sem]))
        out[-1].start()

    for p in range(PIECES):
        first = p * piece
        if p == 0:
            coefficients(0, 2 * piece)
        if p == 2:
            for copy in copies[4:7]:
                copy.wait()
            coefficients(2 * piece, STREAMED)
        state = lax.fori_loop(first // 2, (first + piece) // 2, lambda h, s: steps(2 * h + 1, steps(2 * h, s)), state)
        extra = 0
        if p == PIECES - 1:
            extra = 16 * vregs
            for v in range(2 * vregs):
                u_ref[PIECES * size + 8 * v : PIECES * size + 8 * v + 8, :] = state[v]
        span = pl.ds(p * size, size + extra)
        send(u_ref.at[span], u_hbm.at[span], 10 + p)
    for copy in copies[7:]:
        copy.wait()
    coefficients(STREAMED, chunks)
    send(rows_ref, rows_hbm, 10 + PIECES)
    for copy in out:
        copy.wait()


def legendre_rows(n_dev, lats):
    pairs = LMAX // (2 * n_dev)
    vregs = lats * pairs // (8 * LANES)
    total = step_blocks(n_dev) * n_dev
    cut = STREAMED * CHUNK
    tables = [jnp.asarray(t) for t in recurrence_tables(n_dev, lats)]
    rows = jax.ShapeDtypeStruct((2 * total, LANES), F32)
    u = jax.ShapeDtypeStruct((cut * 4 * vregs + 16 * vregs, LANES), F32)
    return pl.pallas_call(
        functools.partial(recurrence_kernel, n_dev, vregs, float(2 * lats * CYCLE_PIX)),
        out_shape=(rows, u),
        in_specs=[ANY] * 4,
        out_specs=(ANY, ANY),
        scratch_shapes=[pltpu.VMEM(t.shape, t.dtype) for t in [*tables, rows, u]]
        + [pltpu.SemaphoreType.DMA((11 + PIECES,))],
        compiler_params=pltpu.CompilerParams(vmem_limit_bytes=VMEM_LIMIT),
        cost_estimate=pl.CostEstimate(flops=total * 8 * LANES * vregs * 8, bytes_accessed=25000000, transcendentals=0),
        name="legendre_rows",
    )(*tables)


def power_tables(n_dev, n_blk, lats, slots):
    pairs = LMAX // (2 * n_dev)
    cycles_all = 2 * lats
    n_mblk = n_dev // n_blk
    cycle_dev = slots // SEGS
    r_band = cycle_dev * n_mblk
    col = 2 * n_blk * cycle_dev
    pick = np.zeros((4 * lats + 16, n_dev * col))

    def put(row, cycle, phase, weight):
        band, inner = divmod(cycle, r_band)
        j, k = divmod(inner, cycle_dev)
        for s in range(n_blk):
            pick[row, (s * n_mblk + j) * col + (band * cycle_dev + k) * 2 + phase] += weight

    for phase in range(2):
        for n in range(lats):
            for odd in range(2):
                row = (2 * phase + odd) * lats + n
                put(row, n, phase, 1.0)
                if n:
                    put(row, cycles_all - n, phase, -1.0 if odd else 1.0)
        put(4 * lats + phase, lats, phase, 1.0)

    lane = np.arange(LANES)
    band_of = (3 * pairs - 2 - lane) % LANES
    copies = LANES // n_dev
    spread = (band_of[None, :] % copies == (lane // n_dev)[:, None]) & (band_of[None, :] < 2 * pairs)
    gather = band_of[None, :] // copies == np.arange(LMAX // LANES)[:, None]
    return (
        pick.astype(jnp.bfloat16),
        recurrence_tables(n_dev, lats)[3],
        spread.astype(np.float32),
        gather.astype(jnp.bfloat16),
    )


def exact_dot(zero_one, x, dims):
    total = None
    for _ in range(3):
        part = x.astype(BF16)
        x = x - part.astype(F32)
        term = lax.dot_general(zero_one, part, (dims, ((), ())), preferred_element_type=F32)
        total = term if total is None else total + term
    return total


def power_kernel(
    n_dev,
    vregs,
    rows_hbm,
    u_hbm,
    got_ref,
    pick_ref,
    x_ref,
    spread_ref,
    gather_ref,
    out_ref,
    rows_ref,
    u_ref,
    f_ref,
    prod_a,
    prod_b,
    sum_ref,
    accl_ref,
    acch_ref,
    sems,
):
    pairs = LMAX // (2 * n_dev)
    all_steps = step_blocks(n_dev) * n_dev
    cut = STREAMED * CHUNK
    size = cut // PIECES * 4 * vregs
    spans = [pl.ds(p * size, size) for p in range(PIECES)]
    states, coefs = pl.ds(PIECES * size, 16 * vregs), pl.ds(cut, all_steps - cut)
    early, weights = pl.ds(0, cut), pl.ds(all_steps, all_steps)
    copies = fetch(
        [
            (u_hbm.at[states], u_ref.at[states]),
            (rows_hbm.at[coefs], rows_ref.at[coefs]),
        ],
        sems,
    )
    d = device_index()
    reps = LANES // pairs
    lats = vregs * 8 * reps
    per_block = n_dev // CHUNK
    blocks = step_blocks(n_dev)
    chunks = blocks * per_block
    lane = lax.broadcasted_iota(jnp.int32, (8, LANES), 1)
    sub = lax.broadcasted_iota(jnp.int32, (8, LANES), 0)
    q = lax.rem(lane, pairs)
    head = lane < pairs
    sign = jnp.where(sub % 4 == 0, 1.0, jnp.where(sub % 4 == 2, -1.0, 0.0)).astype(F32)
    accl_ref[...] = jnp.zeros_like(accl_ref)
    acch_ref[...] = jnp.zeros_like(acch_ref)
    prod_b[...] = jnp.zeros_like(prod_b)

    f_all = exact_dot(pick_ref[...], got_ref[...], ((1,), (0,)))

    def store(slot, value):
        f_ref[8 * slot : 8 * slot + 8, :] = value

    def load(slot):
        return f_ref[8 * slot : 8 * slot + 8, :]

    for phase in range(2):
        for odd in range(2):
            for v in range(vregs):
                for part in range(2):
                    pieces = []
                    for h in range(reps):
                        row = (2 * phase + odd) * lats + (v * reps + h) * 8
                        pieces.append(f_all[row : row + 8, part * pairs : (part + 1) * pairs])
                    value = jnp.concatenate(pieces, axis=1)
                    if odd:
                        value = value * x_ref[0, 8 * v : 8 * v + 8, :]
                    store(((phase * 2 + odd) * vregs + v) * 2 + part, value)
    base = 8 * vregs
    for phase in range(2):
        row = f_all[4 * lats + phase : 4 * lats + phase + 1, :]
        if 2 * pairs < LANES:
            row = jnp.concatenate([row, jnp.zeros((1, LANES - 2 * pairs), F32)], axis=1)
        store(base + phase, jnp.broadcast_to(row, (8, LANES)) * sign)

    def spectra_now(chunk):
        is_low = q < lax.div(chunk, per_block)

        def now(o, v, p):
            return jnp.where(is_low, load((o * vregs + v) * 2 + p), load(((2 + o) * vregs + v) * 2 + p))

        return [[[now(o, v, p) for p in range(2)] for v in range(vregs)] for o in range(2)]

    def product(s, u, now, prod_ref):
        for part in range(2):
            value = u[0] * now[s % 2][0][part]
            for v in range(1, vregs):
                value = value + u[v] * now[s % 2][v][part]
            prod_ref[part, pl.ds((s // 8) * 8 * PITCH + s % 8, 8, stride=PITCH), :] = value

    def products(chunk, prod_ref, odd):
        now = spectra_now(chunk)
        start = pl.multiple_of(chunk * (CHUNK * 4 * vregs), CHUNK * 4 * vregs)
        first = pl.multiple_of(chunk * CHUNK, CHUNK)
        _, odd = turn_lanes(chunk, per_block, q, seed_low, odd, odd)
        for s in range(0, CHUNK, 2):
            even = [u_ref[pl.ds(start + 8 * (s // 2 * vregs + v), 8), :] for v in range(vregs)]
            one = rows_ref[pl.ds(first + s, 1), :]
            odd = [one * e - o for e, o in zip(even, odd)]
            product(s, even, now, prod_ref)
            product(s + 1, odd, now, prod_ref)
        return odd

    def steps(chunk, prod_ref, state):
        now = spectra_now(chunk)
        even, odd = turn_lanes(chunk, per_block, q, seed_low, list(state[:vregs]), list(state[vregs:]))
        first = pl.multiple_of(chunk * CHUNK, CHUNK)
        for s in range(0, CHUNK, 2):
            fresh_even, fresh_odd = advance(rows_ref, first + s, even, odd, x2)
            product(s, even, now, prod_ref)
            product(s + 1, fresh_odd, now, prod_ref)
            even, odd = fresh_even, fresh_odd
        return (*even, *odd)

    def reduce(chunk, prod_ref):
        for i in range(CHUNK // 8):
            for part in range(2):
                rows = [prod_ref[part, pl.ds((8 * i + s) * PITCH, 8), :] for s in range(8)]
                while len(rows) > 1:
                    rows = [a + b for a, b in zip(rows[::2], rows[1::2])]
                sum_ref[part, pl.ds(pl.multiple_of(chunk * CHUNK, CHUNK) + 8 * i, 8), :] = rows[0]

    def two_inline(h, state):
        state = steps(2 * h, prod_a, state)
        reduce(jnp.maximum(2 * h - 1, STREAMED), prod_b)
        state = steps(2 * h + 1, prod_b, state)
        reduce(2 * h, prod_a)
        return state

    def two_streamed(h, odd):
        odd = products(2 * h, prod_a, list(odd))
        reduce(jnp.maximum(2 * h - 1, 0), prod_b)
        odd = products(2 * h + 1, prod_b, odd)
        reduce(2 * h, prod_a)
        return tuple(odd)

    m_low = (d + n_dev * q).astype(F32)
    x2 = [x_ref[1, 8 * v : 8 * v + 8, :] for v in range(vregs)]
    seed_low = [jnp.exp(m_low * x_ref[2, 8 * v : 8 * v + 8, :]) for v in range(vregs)]
    for copy in copies:
        copy.wait()
    moved = [(rows_hbm.at[early], rows_ref.at[early])] + [(u_hbm.at[span], u_ref.at[span]) for span in spans]
    moved.append((rows_hbm.at[weights], rows_ref.at[weights]))
    copies = [pltpu.make_async_copy(src, dst, sems.at[2 + i]) for i, (src, dst) in enumerate(moved)]
    for copy in copies:
        copy.start()
    state = [u_ref[PIECES * size + 8 * v : PIECES * size + 8 * v + 8, :] for v in range(2 * vregs)]
    lax.fori_loop(STREAMED // 2, chunks // 2, two_inline, tuple(state), unroll=True)
    reduce(chunks - 1, prod_b)
    piece = STREAMED // PIECES
    odd = (jnp.zeros((8, LANES), F32),) * vregs
    copies[0].wait()
    for p in range(PIECES):
        copies[1 + p].wait()
        odd = lax.fori_loop(p * piece // 2, (p + 1) * piece // 2, two_streamed, odd)
    reduce(STREAMED - 1, prod_b)
    copies[-1].wait()

    def packed(tau):
        re, im = sum_ref[0, pl.ds(tau, 8), :], sum_ref[1, pl.ds(tau, 8), :]
        if 2 * pairs == LANES:
            return jnp.where(head, re, im) + pltpu.roll(jnp.where(head, im, re), pairs, 1)
        step = pairs
        while step < LANES:
            re, im = re + pltpu.roll(re, step, 1), im + pltpu.roll(im, step, 1)
            step *= 2
        return jnp.where(head, re, jnp.where(lane < 2 * pairs, im, 0.0))

    def powers(first, count, with_high):
        tiles = n_dev // 8
        places = [(i, j) for j in range(count) for i in range(tiles)]
        taus = [pl.multiple_of((first + j) * n_dev, n_dev) + 8 * i for i, j in places]
        lows = [q < first + j for j in range(count)]
        flats = [load(base)] * count
        if with_high:
            flats = [jnp.where(low, load(base), load(base + 1)) for low in lows]
        values = [packed(tau) for tau in taus]
        values = [v + flats[j] for v, (_, j) in zip(values, places)]
        values = [v * v * rows_ref[pl.ds(all_steps + tau, 8), :] for v, tau in zip(values, taus)]
        low_parts = values
        if with_high:
            low_parts = [jnp.where(lows[j], v, 0.0) for v, (_, j) in zip(values, places)]
            high_parts = [v - low for v, low in zip(values, low_parts)]
        sums = [jnp.sum(v, axis=1, keepdims=True) for v in low_parts]
        if with_high:
            shifts = [count - 1 - j for _, j in places]
            high_parts = [pltpu.roll(v, shift, 1) if shift else v for v, shift in zip(high_parts, shifts)]
        for i in range(tiles):
            total = accl_ref[8 * i : 8 * i + 8, :]
            for j in range(count):
                target = lax.rem(3 * pairs - 1 - (first + j) + 2 * LANES, LANES)
                total = total + jnp.where(lane == target, sums[j * tiles + i], 0.0)
            accl_ref[8 * i : 8 * i + 8, :] = total
            if with_high:
                total = pltpu.roll(acch_ref[8 * i : 8 * i + 8, :], count, 1)
                for j in range(count):
                    total = total + high_parts[j * tiles + i]
                acch_ref[8 * i : 8 * i + 8, :] = total

    many = 512 // n_dev
    half = pairs // many

    def both_halves(g, carry):
        powers(g * many, many, True)
        return carry

    def low_half(g, carry):
        powers(g * many, many, False)
        return carry

    lax.fori_loop(0, half, both_halves, 0)
    lax.fori_loop(half, blocks // many, low_half, 0)
    if blocks % many:
        powers(jnp.int32(blocks - blocks % many), blocks % many, False)

    rows = lax.broadcasted_iota(jnp.int32, (n_dev, LANES), 0)

    def shifted(acc, shift):
        rolled = pltpu.roll(acc, shift, 0)
        return jnp.where(rows < shift, pltpu.roll(rolled, LANES - 1, 1), rolled)

    lanes = lax.broadcasted_iota(jnp.int32, (n_dev, LANES), 1)
    high = acch_ref[...] + pltpu.roll(acch_ref[...], LANES - pairs, 1)
    high = jnp.where(jnp.logical_and(lanes >= pairs - 1, lanes < 2 * pairs - 1), high, 0.0)
    power = shifted(accl_ref[...], d) + shifted(high, n_dev - 1 - d)
    tall = jnp.concatenate([power] * (LANES // n_dev), axis=0) * spread_ref[...]
    out_ref[...] = exact_dot(gather_ref[...], tall, ((1,), (1,)))


def power_of_orders(rows, u, got, n_dev, n_blk, lats, slots):
    pairs = LMAX // (2 * n_dev)
    vregs = lats * pairs // (8 * LANES)
    tables = [jnp.asarray(t) for t in power_tables(n_dev, n_blk, lats, slots)]
    prod = pltpu.VMEM((2, CHUNK * PITCH, LANES), F32)
    return pl.pallas_call(
        functools.partial(power_kernel, n_dev, vregs),
        out_shape=jax.ShapeDtypeStruct((LMAX // LANES, LANES), F32),
        in_specs=[ANY] * 2 + [VMEM] * 5,
        out_specs=VMEM,
        scratch_shapes=[pltpu.VMEM(t.shape, t.dtype) for t in [rows, u]]
        + [
            pltpu.VMEM((8 * (8 * vregs + 2), LANES), F32),
            prod,
            prod,
            pltpu.VMEM((2, step_blocks(n_dev) * n_dev, LANES), F32),
            pltpu.VMEM((n_dev, LANES), F32),
            pltpu.VMEM((n_dev, LANES), F32),
            pltpu.SemaphoreType.DMA((4 + PIECES,)),
        ],
        compiler_params=pltpu.CompilerParams(vmem_limit_bytes=POWER_VMEM),
        cost_estimate=pl.CostEstimate(flops=u.size * 4, bytes_accessed=1000000, transcendentals=0),
        name="order_power",
    )(rows, u, got, *tables)


def on_device(pixels, block_ids, block_mask, model_cl):
    n_blk = lax.axis_size("blk")
    n_mblk = lax.axis_size("mblk")
    n_dev = n_blk * n_mblk
    slots = pixels.shape[0]
    cycles = n_blk * slots // SEGS
    lats = slots * n_dev // SEGS // 2
    pairs = LMAX // (2 * n_dev)

    rows, u = legendre_rows(n_dev, lats)
    sent = cycle_spectra(pixels, block_ids, block_mask, n_dev, n_blk)
    got = lax.all_to_all(sent.reshape(n_dev, 2 * cycles, 2 * pairs), ("blk", "mblk"), 0, 0, tiled=True)
    got = got.reshape(n_dev * 2 * cycles, 2 * pairs)
    power = power_of_orders(rows, u, got, n_dev, n_blk, lats, slots)

    for axis, size in (("mblk", n_mblk), ("blk", n_blk)):
        bit = 1
        while bit < size:
            power = power + lax.ppermute(power, axis, [(i, i ^ bit) for i in range(size)])
            bit *= 2
    pseudo_cl = power.reshape(LMAX)
    rel_error = (pseudo_cl - model_cl) / model_cl
    misfit = jnp.mean(rel_error * rel_error)
    return (pseudo_cl, misfit)


def solution(mesh):
    in_specs = (P(("blk", "mblk"), None), P(("blk", "mblk")), P(("blk", "mblk")), P())
    out_specs = (P(), P())
    return jax.shard_map(
        on_device, mesh=mesh, in_specs=in_specs, out_specs=out_specs, check_vma=False
    )
```

```python
import functools
import math

import jax
import jax.numpy as jnp
import numpy as np
from jax import lax
from jax.experimental import pallas as pl
from jax.experimental.pallas import tpu as pltpu
from jax.sharding import PartitionSpec as P

NSIDE = 2048
CYCLE_PIX = 8192
LMAX = 4096
BLOCK_PIX = 1024
SEGS = 8
LANES = 128
CHUNK = 32
PITCH = 12
STREAMED = 96
PIECES = 6
VMEM_LIMIT = 56 * 1024 * 1024
POWER_VMEM = 51 * 1024 * 1024
F32 = jnp.float32
BF16 = jnp.bfloat16
ANY = pl.BlockSpec(memory_space=pl.ANY)
VMEM = pl.BlockSpec(memory_space=pltpu.VMEM)


def device_index():
    return lax.axis_index("blk") * lax.axis_size("mblk") + lax.axis_index("mblk")


def split_table(table):
    high = table.astype(jnp.bfloat16)
    low = (table - high.astype(np.float64)).astype(jnp.bfloat16)
    return high, low


def split(x):
    high = x.astype(BF16)
    return high, (x - high.astype(F32)).astype(BF16)


def dot(a, b):
    return jnp.dot(a, b, preferred_element_type=F32)


def fetch(pairs, sems):
    copies = [pltpu.make_async_copy(src, dst, sems.at[i]) for i, (src, dst) in enumerate(pairs)]
    for copy in copies:
        copy.start()
    return copies


def dft_tables(n_dev):
    width = CYCLE_PIX // n_dev
    pairs = LMAX // (2 * n_dev)
    a = np.arange(n_dev)
    p2 = np.arange(n_dev)
    p1 = np.arange(width)
    one = 2.0 * np.pi * (a[:, None] * p2[None, :] % n_dev) / n_dev
    first = np.concatenate([np.cos(one), -np.sin(one), np.cos(one)[::-1], -np.sin(one)[::-1]])
    high, low = split_table(first)
    first = np.concatenate([high, low, high], axis=1)
    two = 2.0 * np.pi * a[:, None] * p1[None, :] / CYCLE_PIX
    turn = np.stack([np.cos(two), np.sin(two), np.cos(two)[::-1], np.sin(two)[::-1]])
    q = np.arange(pairs)
    second = []
    for i in (q, 2 * pairs - 1 - q):
        angle = 2.0 * np.pi * (p1[:, None] * i[None, :] % width) / width
        cos, sin = np.cos(angle), np.sin(angle)
        second.append(np.concatenate(split_table(np.block([[cos, -sin], [sin, cos]])), axis=1))
    below = a[:, None] + n_dev * q[None, :]
    half = []
    for m in (below, LMAX - 1 - below):
        angle = np.pi * m / CYCLE_PIX
        cos, sin = np.cos(angle), np.sin(angle)
        half.append(np.concatenate([cos, cos], 1))
        half.append(np.concatenate([sin, -sin], 1))
    return first, turn.astype(np.float32), np.stack(second), np.stack(half).astype(np.float32)


def dft_kernel(
    n_dev,
    n_blk,
    ids_hbm,
    mask_hbm,
    pix_hbm,
    first_hbm,
    turn_hbm,
    second_hbm,
    half_hbm,
    out_hbm,
    out_ref,
    x_ref,
    ids_ref,
    mask_ref,
    pix_ref,
    first_ref,
    turn_ref,
    second_ref,
    half_ref,
    sems,
):
    copies = fetch(
        [
            (ids_hbm, ids_ref),
            (mask_hbm, mask_ref),
            (pix_hbm, pix_ref),
            (first_hbm, first_ref),
            (turn_hbm, turn_ref),
            (second_hbm, second_ref),
            (half_hbm, half_ref),
        ],
        sems,
    )
    slots = pix_ref.shape[0]
    cycle_dev = slots // SEGS
    cycles = n_blk * cycle_dev
    r_band = cycle_dev * (n_dev // n_blk)
    own = lax.axis_index("mblk") * cycle_dev
    width = CYCLE_PIX // n_dev
    rows = BLOCK_PIX // width
    pairs = LMAX // (2 * n_dev)
    x_ref[...] = jnp.zeros_like(x_ref)
    for copy in copies[:3]:
        copy.wait()
    for i in range(slots):
        number = ids_ref[i]
        cycle, seg = lax.div(number, SEGS), lax.rem(number, SEGS)
        band = lax.div(cycle, r_band)
        place = band * cycle_dev + cycle - band * r_band - own
        keep = mask_ref[i].astype(F32)
        for h in range(rows):
            x_ref[place, pl.ds(seg * rows + h, 1), :] = pix_ref[i : i + 1, h * width : (h + 1) * width] * keep
    x = jnp.concatenate([x_ref[c] for c in range(cycles)], axis=1)
    x_high, x_low = split(x)
    copies[3].wait()
    y = dot(first_ref[...], jnp.concatenate([x_high, x_high, x_low], axis=0))
    for copy in copies[4:]:
        copy.wait()
    for phase in range(2):
        y_re = y[2 * phase * n_dev : (2 * phase + 1) * n_dev]
        y_im = y[(2 * phase + 1) * n_dev : (2 * phase + 2) * n_dev]
        cos, sin = turn_ref[2 * phase], turn_ref[2 * phase + 1]
        z = []
        for c in range(cycles):
            re, im = y_re[:, c * width : (c + 1) * width], y_im[:, c * width : (c + 1) * width]
            z.append(jnp.concatenate([re * cos + im * sin, im * cos - re * sin], axis=1))
        z_high, z_low = split(jnp.concatenate(z, axis=0))
        table = second_ref[phase]
        both = dot(z_high, table)
        spec_all = both[:, : 2 * pairs] + both[:, 2 * pairs :] + dot(z_low, table[:, : 2 * pairs])
        for c in range(cycles):
            spec = spec_all[c * n_dev : (c + 1) * n_dev]
            if c % 2 == 0:
                if 2 * pairs == LANES:
                    swapped = pltpu.roll(spec, pairs, 1)
                else:
                    swapped = jnp.concatenate([spec[:, pairs:], spec[:, :pairs]], axis=1)
                spec = spec * half_ref[2 * phase] + swapped * half_ref[2 * phase + 1]
            out_ref[pl.ds(2 * c + phase, n_dev, stride=2 * cycles), :] = spec
    send = pltpu.make_async_copy(out_ref, out_hbm, sems.at[7])
    send.start()
    send.wait()


def cycle_spectra(pixels, block_ids, mask, n_dev, n_blk):
    pairs = LMAX // (2 * n_dev)
    cycles = n_blk * pixels.shape[0] // SEGS
    tables = [jnp.asarray(t) for t in dft_tables(n_dev)]
    out = jax.ShapeDtypeStruct((n_dev * 2 * cycles, 2 * pairs), F32)
    return pl.pallas_call(
        functools.partial(dft_kernel, n_dev, n_blk),
        out_shape=out,
        in_specs=[ANY] * 7,
        out_specs=ANY,
        scratch_shapes=[pltpu.VMEM(out.shape, F32), pltpu.VMEM((cycles, n_dev, CYCLE_PIX // n_dev), F32)]
        + [pltpu.SMEM(block_ids.shape, jnp.int32), pltpu.SMEM(mask.shape, jnp.int32)]
        + [pltpu.VMEM(t.shape, t.dtype) for t in [pixels, *tables]]
        + [pltpu.SemaphoreType.DMA((8,))],
        compiler_params=pltpu.CompilerParams(vmem_limit_bytes=VMEM_LIMIT),
        name="cycle_dft",
    )(block_ids, mask, pixels, *tables)


def wallis(count):
    value = np.zeros(count)
    k = np.arange(0, count - 2, 2)
    value[0::2] = np.concatenate([[1.0], np.cumprod((k + 1.0) / (k + 2.0))])[: len(value[0::2])]
    value[1::2] = 2.0 / np.pi * np.concatenate([[1.0], np.cumprod((k + 2.0) / (k + 3.0))])[: len(value[1::2])]
    return value


def step_blocks(n_dev):
    blocks = LMAX // n_dev + 1
    return blocks + blocks * (n_dev // CHUNK) % 2


def latitude_lanes(n_dev, lats):
    pairs = LMAX // (2 * n_dev)
    x = (lats - np.arange(lats)) * (2.0 / (3.0 * NSIDE))
    reps = LANES // pairs
    order = np.arange(lats).reshape(-1, reps, 8)
    return np.repeat(x[order].transpose(0, 2, 1), pairs, axis=2).reshape(-1, LANES)


def recurrence_tables(n_dev, lats):
    pairs = LMAX // (2 * n_dev)
    total = step_blocks(n_dev) * n_dev
    value = wallis(2 * LMAX + 6 * n_dev + total)
    tau = np.arange(total)[:, None]
    q = np.arange(pairs)[None, :]
    rise = np.where(q < tau // n_dev, tau - n_dev * (q + 1), tau)
    wide = np.arange(total + 2 * n_dev)[:, None]
    t_low = value[np.maximum(wide - n_dev + n_dev * q, 0)]
    t_high = value[wide + 2 * LMAX - 2 - 2 * n_dev * q - 2 * (n_dev - 1)]
    x = latitude_lanes(n_dev, lats)
    x_tabs = np.stack([x, x * x, 0.5 * np.log1p(-x * x)])
    tables = [np.tile(t, (1, LANES // pairs)) for t in (value[rise], t_low, t_high)]
    return [t.astype(np.float32) for t in tables + [x_tabs]]


def advance(coef_ref, row, even, odd, x2):
    one, two = coef_ref[pl.ds(row, 1), :], coef_ref[pl.ds(row + 1, 1), :]
    fresh_odd = [one * e - o for e, o in zip(even, odd)]
    gains = [two * x for x in x2]
    fresh_even = [(g * one - 1.0) * e - g * o for g, e, o in zip(gains, even, odd)]
    return fresh_even, fresh_odd


def turn_lanes(chunk, per_block, q, seeds, even, odd):
    turned = q == lax.div(chunk, per_block) - 1
    if per_block > 1:
        turned = jnp.logical_and(turned, lax.rem(chunk, per_block) == 0)
    return [jnp.where(turned, s, e) for s, e in zip(seeds, even)], [jnp.where(turned, 0.0, o) for o in odd]


def recurrence_kernel(
    n_dev,
    vregs,
    pixel_total,
    rise_hbm,
    low_hbm,
    high_hbm,
    x_hbm,
    rows_hbm,
    u_hbm,
    rise_ref,
    low_ref,
    high_ref,
    x_ref,
    rows_ref,
    u_ref,
    even_ref,
    sems,
):
    pairs = LMAX // (2 * n_dev)
    per_block = n_dev // CHUNK
    chunks = step_blocks(n_dev) * per_block
    total = chunks * CHUNK
    piece = STREAMED // PIECES
    ends = [0, 2 * piece * CHUNK, STREAMED * CHUNK, total]
    parts = [(x_hbm, x_ref)]
    for start, stop in zip(ends, ends[1:]):
        for src, dst in ((rise_hbm, rise_ref), (low_hbm, low_ref), (high_hbm, high_ref)):
            reach = 0 if src is rise_hbm else 2 * n_dev
            first = start + reach if start else 0
            span = pl.ds(first, stop + reach - first)
            parts.append((src.at[span], dst.at[span]))
    copies = fetch(parts, sems)
    d = device_index()
    lane = lax.broadcasted_iota(jnp.int32, (8, LANES), 1)
    sub = lax.broadcasted_iota(jnp.int32, (8, LANES), 0)
    q = lax.rem(lane, pairs)
    m_low = (d + n_dev * q).astype(F32)
    m_high = (LMAX - 1.0) - m_low
    weight_low = jnp.where(m_low == 0.0, 1.0, 2.0) / pixel_total
    weight_high = jnp.full((8, LANES), 2.0 / pixel_total, F32)
    l_low = sub.astype(F32) + (d.astype(F32) - n_dev)
    l_high = sub.astype(F32) + m_high
    for copy in copies[:4]:
        copy.wait()
    x2 = [x_ref[1, 8 * v : 8 * v + 8, :] for v in range(vregs)]
    logs = [x_ref[2, 8 * v : 8 * v + 8, :] for v in range(vregs)]
    seed_low = [jnp.exp(m_low * g) for g in logs]
    seed_high = [jnp.exp(m_high * g) for g in logs]

    def coefficients(start, stop):
        many = max(n for n in range(1, 13) if (stop - start) % n == 0)

        def some(group, carry):
            fresh = []
            for step in range(many):
                chunk = start + group * many + step
                is_low = q < lax.div(chunk, per_block)
                weight = jnp.where(is_low, weight_low, weight_high)
                first = jnp.where(is_low, l_low, l_high) + (chunk * CHUNK).astype(F32)
                for i in range(CHUNK // 8):
                    tau = pl.multiple_of(chunk * CHUNK, CHUNK) + 8 * i
                    low = low_ref[pl.ds(tau + 2 * d, 8), :]
                    high = high_ref[pl.ds(tau + 2 * (n_dev - 1 - d), 8), :]
                    product = rise_ref[pl.ds(tau, 8), :] * jnp.where(is_low, low, high)
                    degree = first + 8.0 * i
                    coef = product * (degree * math.pi + 0.5 * math.pi)
                    fresh.append((tau, coef, jnp.where(degree < LMAX, product * weight, 0.0)))
            for tau, coef, weight in fresh:
                rows_ref[pl.ds(tau, 8), :] = coef
                rows_ref[pl.ds(total + tau, 8), :] = weight
            return carry

        lax.fori_loop(0, (stop - start) // many, some, 0)

    def steps(chunk, state):
        even, odd = turn_lanes(chunk, per_block, q, seed_low, list(state[:vregs]), list(state[vregs:]))
        first = pl.multiple_of(chunk * CHUNK, CHUNK)
        start = pl.multiple_of(chunk * (CHUNK * 4 * vregs), CHUNK * 4 * vregs)
        for s in range(0, CHUNK, 2):
            fresh_even, fresh_odd = advance(rows_ref, first + s, even, odd, x2)
            for v in range(vregs):
                u_ref[pl.ds(start + 8 * (s // 2 * vregs + v), 8), :] = even[v]
            even, odd = fresh_even, fresh_odd
        return (*even, *odd)

    zero = jnp.zeros((8, LANES), F32)
    state = (*seed_high, *([zero] * vregs))
    size = piece * CHUNK * 4 * vregs
    out = []

    def send(src, dst, sem):
        out.append(pltpu.make_async_copy(src, dst, sems.at[sem]))
        out[-1].start()

    for p in range(PIECES):
        first = p * piece
        if p == 0:
            coefficients(0, 2 * piece)
        if p == 2:
            for copy in copies[4:7]:
                copy.wait()
            coefficients(2 * piece, STREAMED)
        state = lax.fori_loop(first // 2, (first + piece) // 2, lambda h, s: steps(2 * h + 1, steps(2 * h, s)), state)
        extra = 0
        if p == PIECES - 1:
            extra = 16 * vregs
            for v in range(2 * vregs):
                u_ref[PIECES * size + 8 * v : PIECES * size + 8 * v + 8, :] = state[v]
        span = pl.ds(p * size, size + extra)
        send(u_ref.at[span], u_hbm.at[span], 10 + p)
    cut = STREAMED * CHUNK
    for i in range(cut // 16):
        even_ref[8 * i : 8 * i + 8, :] = rows_ref[pl.ds(16 * i, 8, stride=2), :]
    send(even_ref, rows_hbm.at[pl.ds(0, cut // 2)], 10 + PIECES)
    for copy in copies[7:]:
        copy.wait()
    coefficients(STREAMED, chunks)
    rest = 2 * total - cut
    send(rows_ref.at[pl.ds(cut, rest)], rows_hbm.at[pl.ds(cut // 2, rest)], 11 + PIECES)
    for copy in out:
        copy.wait()


def legendre_rows(n_dev, lats):
    pairs = LMAX // (2 * n_dev)
    vregs = lats * pairs // (8 * LANES)
    total = step_blocks(n_dev) * n_dev
    cut = STREAMED * CHUNK
    tables = [jnp.asarray(t) for t in recurrence_tables(n_dev, lats)]
    rows = jax.ShapeDtypeStruct((2 * total, LANES), F32)
    u = jax.ShapeDtypeStruct((cut * 4 * vregs + 16 * vregs, LANES), F32)
    return pl.pallas_call(
        functools.partial(recurrence_kernel, n_dev, vregs, float(2 * lats * CYCLE_PIX)),
        out_shape=(jax.ShapeDtypeStruct((2 * total - cut // 2, LANES), F32), u),
        in_specs=[ANY] * 4,
        out_specs=(ANY, ANY),
        scratch_shapes=[pltpu.VMEM(t.shape, t.dtype) for t in [*tables, rows, u]]
        + [pltpu.VMEM((cut // 2, LANES), F32), pltpu.SemaphoreType.DMA((12 + PIECES,))],
        compiler_params=pltpu.CompilerParams(vmem_limit_bytes=VMEM_LIMIT),
        cost_estimate=pl.CostEstimate(flops=total * 8 * LANES * vregs * 8, bytes_accessed=25000000, transcendentals=0),
        name="legendre_rows",
    )(*tables)


def power_tables(n_dev, n_blk, lats, slots):
    pairs = LMAX // (2 * n_dev)
    cycles_all = 2 * lats
    n_mblk = n_dev // n_blk
    cycle_dev = slots // SEGS
    r_band = cycle_dev * n_mblk
    col = 2 * n_blk * cycle_dev
    pick = np.zeros((4 * lats + 16, n_dev * col))

    def put(row, cycle, phase, weight):
        band, inner = divmod(cycle, r_band)
        j, k = divmod(inner, cycle_dev)
        for s in range(n_blk):
            pick[row, (s * n_mblk + j) * col + (band * cycle_dev + k) * 2 + phase] += weight

    for phase in range(2):
        for n in range(lats):
            for odd in range(2):
                row = (2 * phase + odd) * lats + n
                put(row, n, phase, 1.0)
                if n:
                    put(row, cycles_all - n, phase, -1.0 if odd else 1.0)
        put(4 * lats + phase, lats, phase, 1.0)

    lane = np.arange(LANES)
    band_of = (3 * pairs - 2 - lane) % LANES
    copies = LANES // n_dev
    spread = (band_of[None, :] % copies == (lane // n_dev)[:, None]) & (band_of[None, :] < 2 * pairs)
    gather = band_of[None, :] // copies == np.arange(LMAX // LANES)[:, None]
    return (
        pick.astype(jnp.bfloat16),
        recurrence_tables(n_dev, lats)[3],
        spread.astype(np.float32),
        gather.astype(jnp.bfloat16),
    )


def exact_dot(zero_one, x, dims):
    total = None
    for _ in range(3):
        part = x.astype(BF16)
        x = x - part.astype(F32)
        term = lax.dot_general(zero_one, part, (dims, ((), ())), preferred_element_type=F32)
        total = term if total is None else total + term
    return total


def power_kernel(
    n_dev,
    vregs,
    rows_hbm,
    u_hbm,
    got_ref,
    pick_ref,
    x_ref,
    spread_ref,
    gather_ref,
    out_ref,
    rows_ref,
    u_ref,
    f_ref,
    prod_a,
    prod_b,
    sum_ref,
    accl_ref,
    acch_ref,
    sems,
):
    pairs = LMAX // (2 * n_dev)
    all_steps = step_blocks(n_dev) * n_dev
    cut = STREAMED * CHUNK
    size = cut // PIECES * 4 * vregs
    spans = [pl.ds(p * size, size) for p in range(PIECES)]
    states, soon = pl.ds(PIECES * size, 16 * vregs), pl.ds(cut // 2, 8 * CHUNK)
    later = pl.ds(cut // 2 + 8 * CHUNK, all_steps - cut - 8 * CHUNK)
    early, weights = pl.ds(0, cut // 2), pl.ds(all_steps - cut // 2, all_steps)
    copies = fetch(
        [
            (u_hbm.at[states], u_ref.at[states]),
            (rows_hbm.at[soon], rows_ref.at[soon]),
        ],
        sems,
    )
    d = device_index()
    reps = LANES // pairs
    lats = vregs * 8 * reps
    per_block = n_dev // CHUNK
    blocks = step_blocks(n_dev)
    chunks = blocks * per_block
    lane = lax.broadcasted_iota(jnp.int32, (8, LANES), 1)
    sub = lax.broadcasted_iota(jnp.int32, (8, LANES), 0)
    q = lax.rem(lane, pairs)
    head = lane < pairs
    sign = jnp.where(sub % 4 == 0, 1.0, jnp.where(sub % 4 == 2, -1.0, 0.0)).astype(F32)
    accl_ref[...] = jnp.zeros_like(accl_ref)
    acch_ref[...] = jnp.zeros_like(acch_ref)
    prod_b[...] = jnp.zeros_like(prod_b)

    f_all = exact_dot(pick_ref[...], got_ref[...], ((1,), (0,)))

    def store(slot, value):
        f_ref[8 * slot : 8 * slot + 8, :] = value

    def load(slot):
        return f_ref[8 * slot : 8 * slot + 8, :]

    for phase in range(2):
        for odd in range(2):
            for v in range(vregs):
                for part in range(2):
                    pieces = []
                    for h in range(reps):
                        row = (2 * phase + odd) * lats + (v * reps + h) * 8
                        pieces.append(f_all[row : row + 8, part * pairs : (part + 1) * pairs])
                    value = jnp.concatenate(pieces, axis=1)
                    if odd:
                        value = value * x_ref[0, 8 * v : 8 * v + 8, :]
                    store(((phase * 2 + odd) * vregs + v) * 2 + part, value)
    base = 8 * vregs
    for phase in range(2):
        row = f_all[4 * lats + phase : 4 * lats + phase + 1, :]
        if 2 * pairs < LANES:
            row = jnp.concatenate([row, jnp.zeros((1, LANES - 2 * pairs), F32)], axis=1)
        store(base + phase, jnp.broadcast_to(row, (8, LANES)) * sign)

    def spectra_now(chunk):
        is_low = q < lax.div(chunk, per_block)

        def now(o, v, p):
            return jnp.where(is_low, load((o * vregs + v) * 2 + p), load(((2 + o) * vregs + v) * 2 + p))

        return [[[now(o, v, p) for p in range(2)] for v in range(vregs)] for o in range(2)]

    def product(s, u, now, prod_ref):
        for part in range(2):
            value = u[0] * now[s % 2][0][part]
            for v in range(1, vregs):
                value = value + u[v] * now[s % 2][v][part]
            prod_ref[part, pl.ds((s // 8) * 8 * PITCH + s % 8, 8, stride=PITCH), :] = value

    def products(chunk, prod_ref, odd):
        now = spectra_now(chunk)
        start = pl.multiple_of(chunk * (CHUNK * 4 * vregs), CHUNK * 4 * vregs)
        first = pl.multiple_of(chunk * (CHUNK // 2), CHUNK // 2)
        _, odd = turn_lanes(chunk, per_block, q, seed_low, odd, odd)
        for s in range(0, CHUNK, 2):
            even = [u_ref[pl.ds(start + 8 * (s // 2 * vregs + v), 8), :] for v in range(vregs)]
            one = rows_ref[pl.ds(first + s // 2, 1), :]
            odd = [one * e - o for e, o in zip(even, odd)]
            product(s, even, now, prod_ref)
            product(s + 1, odd, now, prod_ref)
        return odd

    def steps(chunk, prod_ref, state):
        now = spectra_now(chunk)
        even, odd = turn_lanes(chunk, per_block, q, seed_low, list(state[:vregs]), list(state[vregs:]))
        first = pl.multiple_of(chunk * CHUNK - cut // 2, CHUNK // 2)
        for s in range(0, CHUNK, 2):
            fresh_even, fresh_odd = advance(rows_ref, first + s, even, odd, x2)
            product(s, even, now, prod_ref)
            product(s + 1, fresh_odd, now, prod_ref)
            even, odd = fresh_even, fresh_odd
        return (*even, *odd)

    def reduce(chunk, prod_ref):
        for i in range(CHUNK // 8):
            for part in range(2):
                rows = [prod_ref[part, pl.ds((8 * i + s) * PITCH, 8), :] for s in range(8)]
                while len(rows) > 1:
                    rows = [a + b for a, b in zip(rows[::2], rows[1::2])]
                sum_ref[part, pl.ds(pl.multiple_of(chunk * CHUNK, CHUNK) + 8 * i, 8), :] = rows[0]

    def two_inline(h, state):
        state = steps(2 * h, prod_a, state)
        reduce(jnp.maximum(2 * h - 1, STREAMED), prod_b)
        state = steps(2 * h + 1, prod_b, state)
        reduce(2 * h, prod_a)
        return state

    def two_streamed(h, odd):
        odd = products(2 * h, prod_a, list(odd))
        reduce(jnp.maximum(2 * h - 1, 0), prod_b)
        odd = products(2 * h + 1, prod_b, odd)
        reduce(2 * h, prod_a)
        return tuple(odd)

    m_low = (d + n_dev * q).astype(F32)
    x2 = [x_ref[1, 8 * v : 8 * v + 8, :] for v in range(vregs)]
    seed_low = [jnp.exp(m_low * x_ref[2, 8 * v : 8 * v + 8, :]) for v in range(vregs)]
    for copy in copies:
        copy.wait()
    moved = [(rows_hbm.at[span], rows_ref.at[span]) for span in (later, early)] + [(u_hbm.at[span], u_ref.at[span]) for span in spans]
    moved.append((rows_hbm.at[weights], rows_ref.at[weights]))
    copies = [pltpu.make_async_copy(src, dst, sems.at[2 + i]) for i, (src, dst) in enumerate(moved)]
    for copy in copies:
        copy.start()
    state = [u_ref[PIECES * size + 8 * v : PIECES * size + 8 * v + 8, :] for v in range(2 * vregs)]
    state = lax.fori_loop(STREAMED // 2, STREAMED // 2 + 4, two_inline, tuple(state), unroll=True)
    copies[0].wait()
    lax.fori_loop(STREAMED // 2 + 4, chunks // 2, two_inline, tuple(state), unroll=True)
    reduce(chunks - 1, prod_b)
    piece = STREAMED // PIECES
    odd = (jnp.zeros((8, LANES), F32),) * vregs
    copies[1].wait()
    for p in range(PIECES):
        copies[2 + p].wait()
        odd = lax.fori_loop(p * piece // 2, (p + 1) * piece // 2, two_streamed, odd)
    reduce(STREAMED - 1, prod_b)
    copies[-1].wait()

    def packed(tau):
        re, im = sum_ref[0, pl.ds(tau, 8), :], sum_ref[1, pl.ds(tau, 8), :]
        if 2 * pairs == LANES:
            return jnp.where(head, re, im) + pltpu.roll(jnp.where(head, im, re), pairs, 1)
        step = pairs
        while step < LANES:
            re, im = re + pltpu.roll(re, step, 1), im + pltpu.roll(im, step, 1)
            step *= 2
        return jnp.where(head, re, jnp.where(lane < 2 * pairs, im, 0.0))

    def powers(first, count, with_high):
        tiles = n_dev // 8
        places = [(i, j) for j in range(count) for i in range(tiles)]
        taus = [pl.multiple_of((first + j) * n_dev, n_dev) + 8 * i for i, j in places]
        lows = [q < first + j for j in range(count)]
        flats = [load(base)] * count
        if with_high:
            flats = [jnp.where(low, load(base), load(base + 1)) for low in lows]
        values = [packed(tau) for tau in taus]
        values = [v + flats[j] for v, (_, j) in zip(values, places)]
        values = [v * v * rows_ref[pl.ds(all_steps - cut // 2 + tau, 8), :] for v, tau in zip(values, taus)]
        low_parts = values
        if with_high:
            low_parts = [jnp.where(lows[j], v, 0.0) for v, (_, j) in zip(values, places)]
            high_parts = [v - low for v, low in zip(values, low_parts)]
        sums = [jnp.sum(v, axis=1, keepdims=True) for v in low_parts]
        if with_high:
            shifts = [count - 1 - j for _, j in places]
            high_parts = [pltpu.roll(v, shift, 1) if shift else v for v, shift in zip(high_parts, shifts)]
        for i in range(tiles):
            total = accl_ref[8 * i : 8 * i + 8, :]
            for j in range(count):
                target = lax.rem(3 * pairs - 1 - (first + j) + 2 * LANES, LANES)
                total = total + jnp.where(lane == target, sums[j * tiles + i], 0.0)
            accl_ref[8 * i : 8 * i + 8, :] = total
            if with_high:
                total = pltpu.roll(acch_ref[8 * i : 8 * i + 8, :], count, 1)
                for j in range(count):
                    total = total + high_parts[j * tiles + i]
                acch_ref[8 * i : 8 * i + 8, :] = total

    many = 1024 // n_dev
    half = pairs // many

    def both_halves(g, carry):
        powers(g * many, many, True)
        return carry

    def low_half(g, carry):
        powers(g * many, many, False)
        return carry

    lax.fori_loop(0, half, both_halves, 0)
    lax.fori_loop(half, blocks // many, low_half, 0)
    if blocks % many:
        powers(jnp.int32(blocks - blocks % many), blocks % many, False)

    rows = lax.broadcasted_iota(jnp.int32, (n_dev, LANES), 0)

    def shifted(acc, shift):
        rolled = pltpu.roll(acc, shift, 0)
        return jnp.where(rows < shift, pltpu.roll(rolled, LANES - 1, 1), rolled)

    lanes = lax.broadcasted_iota(jnp.int32, (n_dev, LANES), 1)
    high = acch_ref[...] + pltpu.roll(acch_ref[...], LANES - pairs, 1)
    high = jnp.where(jnp.logical_and(lanes >= pairs - 1, lanes < 2 * pairs - 1), high, 0.0)
    power = shifted(accl_ref[...], d) + shifted(high, n_dev - 1 - d)
    tall = jnp.concatenate([power] * (LANES // n_dev), axis=0) * spread_ref[...]
    out_ref[...] = exact_dot(gather_ref[...], tall, ((1,), (1,)))


def power_of_orders(rows, u, got, n_dev, n_blk, lats, slots):
    pairs = LMAX // (2 * n_dev)
    vregs = lats * pairs // (8 * LANES)
    tables = [jnp.asarray(t) for t in power_tables(n_dev, n_blk, lats, slots)]
    prod = pltpu.VMEM((2, CHUNK * PITCH, LANES), F32)
    return pl.pallas_call(
        functools.partial(power_kernel, n_dev, vregs),
        out_shape=jax.ShapeDtypeStruct((LMAX // LANES, LANES), F32),
        in_specs=[ANY] * 2 + [VMEM] * 5,
        out_specs=VMEM,
        scratch_shapes=[pltpu.VMEM(t.shape, t.dtype) for t in [rows, u]]
        + [
            pltpu.VMEM((8 * (8 * vregs + 2), LANES), F32),
            prod,
            prod,
            pltpu.VMEM((2, step_blocks(n_dev) * n_dev, LANES), F32),
            pltpu.VMEM((n_dev, LANES), F32),
            pltpu.VMEM((n_dev, LANES), F32),
            pltpu.SemaphoreType.DMA((5 + PIECES,)),
        ],
        compiler_params=pltpu.CompilerParams(vmem_limit_bytes=POWER_VMEM),
        cost_estimate=pl.CostEstimate(flops=u.size * 4, bytes_accessed=1000000, transcendentals=0),
        name="order_power",
    )(rows, u, got, *tables)


def finish_kernel(own_ref, other_ref, model_ref, cl_ref, misfit_ref):
    cl = own_ref[...] + other_ref[...]
    model = model_ref[...]
    cl_ref[...] = cl
    error = (cl - model) / model
    squares = jnp.sum(error * error, axis=0, keepdims=True)
    misfit_ref[...] = jnp.sum(squares, axis=1, keepdims=True) * (1.0 / LMAX)


def finish(own, other, model_cl):
    cl, misfit = pl.pallas_call(
        finish_kernel,
        out_shape=(jax.ShapeDtypeStruct(own.shape, F32), jax.ShapeDtypeStruct((1, 1), F32)),
        in_specs=[VMEM] * 3,
        out_specs=(VMEM, VMEM),
        compiler_params=pltpu.CompilerParams(vmem_limit_bytes=2 * 1024 * 1024),
        name="finish",
    )(own, other, model_cl.reshape(own.shape))
    return cl.reshape(LMAX), misfit.reshape(())


def on_device(pixels, block_ids, block_mask, model_cl):
    n_blk = lax.axis_size("blk")
    n_mblk = lax.axis_size("mblk")
    n_dev = n_blk * n_mblk
    slots = pixels.shape[0]
    cycles = n_blk * slots // SEGS
    lats = slots * n_dev // SEGS // 2
    pairs = LMAX // (2 * n_dev)

    rows, u = legendre_rows(n_dev, lats)
    sent = cycle_spectra(pixels, block_ids, block_mask, n_dev, n_blk)
    got = lax.all_to_all(sent.reshape(n_dev, 2 * cycles, 2 * pairs), ("blk", "mblk"), 0, 0, tiled=True)
    got = got.reshape(n_dev * 2 * cycles, 2 * pairs)
    power = power_of_orders(rows, u, got, n_dev, n_blk, lats, slots)

    other = jnp.zeros_like(power)
    for axis, size in (("mblk", n_mblk), ("blk", n_blk)):
        bit = 1
        while bit < size:
            power = power + other
            other = lax.ppermute(power, axis, [(i, i ^ bit) for i in range(size)])
            bit *= 2
    return finish(power, other, model_cl)


def solution(mesh):
    in_specs = (P(("blk", "mblk"), None), P(("blk", "mblk")), P(("blk", "mblk")), P())
    out_specs = (P(), P())
    return jax.shard_map(
        on_device, mesh=mesh, in_specs=in_specs, out_specs=out_specs, check_vma=False
    )
```

```python
import functools
import math

import jax
import jax.numpy as jnp
import numpy as np
from jax import lax
from jax.experimental import pallas as pl
from jax.experimental.pallas import tpu as pltpu
from jax.sharding import PartitionSpec as P

NSIDE = 2048
CYCLE_PIX = 8192
LMAX = 4096
BLOCK_PIX = 1024
SEGS = 8
LANES = 128
CHUNK = 32
PITCH = 12
STREAMED = 96
PIECES = 6
VMEM_LIMIT = 56 * 1024 * 1024
POWER_VMEM = 51 * 1024 * 1024
F32 = jnp.float32
BF16 = jnp.bfloat16
ANY = pl.BlockSpec(memory_space=pl.ANY)
VMEM = pl.BlockSpec(memory_space=pltpu.VMEM)


def device_index():
    return lax.axis_index("blk") * lax.axis_size("mblk") + lax.axis_index("mblk")


def split_table(table):
    high = table.astype(jnp.bfloat16)
    low = (table - high.astype(np.float64)).astype(jnp.bfloat16)
    return high, low


def split(x):
    high = x.astype(BF16)
    return high, (x - high.astype(F32)).astype(BF16)


def dot(a, b):
    return jnp.dot(a, b, preferred_element_type=F32)


def fetch(pairs, sems):
    copies = [pltpu.make_async_copy(src, dst, sems.at[i]) for i, (src, dst) in enumerate(pairs)]
    for copy in copies:
        copy.start()
    return copies


def dft_tables(n_dev):
    width = CYCLE_PIX // n_dev
    pairs = LMAX // (2 * n_dev)
    a = np.arange(n_dev)
    p2 = np.arange(n_dev)
    p1 = np.arange(width)
    one = 2.0 * np.pi * (a[:, None] * p2[None, :] % n_dev) / n_dev
    first = np.concatenate([np.cos(one), -np.sin(one), np.cos(one)[::-1], -np.sin(one)[::-1]])
    high, low = split_table(first)
    first = np.concatenate([high, low, high], axis=1)
    two = 2.0 * np.pi * a[:, None] * p1[None, :] / CYCLE_PIX
    turn = np.stack([np.cos(two), np.sin(two), np.cos(two)[::-1], np.sin(two)[::-1]])
    q = np.arange(pairs)
    second = []
    for i in (q, 2 * pairs - 1 - q):
        angle = 2.0 * np.pi * (p1[:, None] * i[None, :] % width) / width
        cos, sin = np.cos(angle), np.sin(angle)
        second.append(np.concatenate(split_table(np.block([[cos, -sin], [sin, cos]])), axis=1))
    below = a[:, None] + n_dev * q[None, :]
    half = []
    for m in (below, LMAX - 1 - below):
        angle = np.pi * m / CYCLE_PIX
        cos, sin = np.cos(angle), np.sin(angle)
        half.append(np.concatenate([cos, cos], 1))
        half.append(np.concatenate([sin, -sin], 1))
    return first, turn.astype(np.float32), np.stack(second), np.stack(half).astype(np.float32)


def dft_kernel(
    n_dev,
    n_blk,
    ids_hbm,
    mask_hbm,
    pix_hbm,
    first_hbm,
    turn_hbm,
    second_hbm,
    half_hbm,
    out_hbm,
    out_ref,
    x_ref,
    ids_ref,
    mask_ref,
    pix_ref,
    first_ref,
    turn_ref,
    second_ref,
    half_ref,
    sems,
):
    copies = fetch(
        [
            (ids_hbm, ids_ref),
            (mask_hbm, mask_ref),
            (pix_hbm, pix_ref),
            (first_hbm, first_ref),
            (turn_hbm, turn_ref),
            (second_hbm, second_ref),
            (half_hbm, half_ref),
        ],
        sems,
    )
    slots = pix_ref.shape[0]
    cycle_dev = slots // SEGS
    cycles = n_blk * cycle_dev
    r_band = cycle_dev * (n_dev // n_blk)
    own = lax.axis_index("mblk") * cycle_dev
    width = CYCLE_PIX // n_dev
    rows = BLOCK_PIX // width
    pairs = LMAX // (2 * n_dev)
    x_ref[...] = jnp.zeros_like(x_ref)
    for copy in copies[:3]:
        copy.wait()
    for i in range(slots):
        number = ids_ref[i]
        cycle, seg = lax.div(number, SEGS), lax.rem(number, SEGS)
        band = lax.div(cycle, r_band)
        place = band * cycle_dev + cycle - band * r_band - own
        keep = mask_ref[i].astype(F32)
        for h in range(rows):
            x_ref[place, pl.ds(seg * rows + h, 1), :] = pix_ref[i : i + 1, h * width : (h + 1) * width] * keep
    x = jnp.concatenate([x_ref[c] for c in range(cycles)], axis=1)
    x_high, x_low = split(x)
    copies[3].wait()
    y = dot(first_ref[...], jnp.concatenate([x_high, x_high, x_low], axis=0))
    for copy in copies[4:]:
        copy.wait()
    for phase in range(2):
        y_re = y[2 * phase * n_dev : (2 * phase + 1) * n_dev]
        y_im = y[(2 * phase + 1) * n_dev : (2 * phase + 2) * n_dev]
        cos, sin = turn_ref[2 * phase], turn_ref[2 * phase + 1]
        z = []
        for c in range(cycles):
            re, im = y_re[:, c * width : (c + 1) * width], y_im[:, c * width : (c + 1) * width]
            z.append(jnp.concatenate([re * cos + im * sin, im * cos - re * sin], axis=1))
        z_high, z_low = split(jnp.concatenate(z, axis=0))
        table = second_ref[phase]
        both = dot(z_high, table)
        spec_all = both[:, : 2 * pairs] + both[:, 2 * pairs :] + dot(z_low, table[:, : 2 * pairs])
        for c in range(cycles):
            spec = spec_all[c * n_dev : (c + 1) * n_dev]
            if c % 2 == 0:
                if 2 * pairs == LANES:
                    swapped = pltpu.roll(spec, pairs, 1)
                else:
                    swapped = jnp.concatenate([spec[:, pairs:], spec[:, :pairs]], axis=1)
                spec = spec * half_ref[2 * phase] + swapped * half_ref[2 * phase + 1]
            out_ref[pl.ds(2 * c + phase, n_dev, stride=2 * cycles), :] = spec
    send = pltpu.make_async_copy(out_ref, out_hbm, sems.at[7])
    send.start()
    send.wait()


def cycle_spectra(pixels, block_ids, mask, n_dev, n_blk):
    pairs = LMAX // (2 * n_dev)
    cycles = n_blk * pixels.shape[0] // SEGS
    tables = [jnp.asarray(t) for t in dft_tables(n_dev)]
    out = jax.ShapeDtypeStruct((n_dev * 2 * cycles, 2 * pairs), F32)
    return pl.pallas_call(
        functools.partial(dft_kernel, n_dev, n_blk),
        out_shape=out,
        in_specs=[ANY] * 7,
        out_specs=ANY,
        scratch_shapes=[pltpu.VMEM(out.shape, F32), pltpu.VMEM((cycles, n_dev, CYCLE_PIX // n_dev), F32)]
        + [pltpu.SMEM(block_ids.shape, jnp.int32), pltpu.SMEM(mask.shape, jnp.int32)]
        + [pltpu.VMEM(t.shape, t.dtype) for t in [pixels, *tables]]
        + [pltpu.SemaphoreType.DMA((8,))],
        compiler_params=pltpu.CompilerParams(vmem_limit_bytes=VMEM_LIMIT),
        name="cycle_dft",
    )(block_ids, mask, pixels, *tables)


def wallis(count):
    value = np.zeros(count)
    k = np.arange(0, count - 2, 2)
    value[0::2] = np.concatenate([[1.0], np.cumprod((k + 1.0) / (k + 2.0))])[: len(value[0::2])]
    value[1::2] = 2.0 / np.pi * np.concatenate([[1.0], np.cumprod((k + 2.0) / (k + 3.0))])[: len(value[1::2])]
    return value


def step_blocks(n_dev):
    blocks = LMAX // n_dev + 1
    return blocks + blocks * (n_dev // CHUNK) % 2


def latitude_lanes(n_dev, lats):
    pairs = LMAX // (2 * n_dev)
    x = (lats - np.arange(lats)) * (2.0 / (3.0 * NSIDE))
    reps = LANES // pairs
    order = np.arange(lats).reshape(-1, reps, 8)
    return np.repeat(x[order].transpose(0, 2, 1), pairs, axis=2).reshape(-1, LANES)


def recurrence_tables(n_dev, lats):
    pairs = LMAX // (2 * n_dev)
    total = step_blocks(n_dev) * n_dev
    value = wallis(2 * LMAX + 6 * n_dev + total)
    tau = np.arange(total)[:, None]
    q = np.arange(pairs)[None, :]
    rise = np.where(q < tau // n_dev, tau - n_dev * (q + 1), tau)
    wide = np.arange(total + 2 * n_dev)[:, None]
    t_low = value[np.maximum(wide - n_dev + n_dev * q, 0)]
    t_high = value[wide + 2 * LMAX - 2 - 2 * n_dev * q - 2 * (n_dev - 1)]
    x = latitude_lanes(n_dev, lats)
    x_tabs = np.stack([x, x * x, 0.5 * np.log1p(-x * x)])
    tables = [np.tile(t, (1, LANES // pairs)) for t in (value[rise], t_low, t_high)]
    return [t.astype(np.float32) for t in tables + [x_tabs]]


def advance(coef_ref, row, even, odd, x2):
    one, two = coef_ref[pl.ds(row, 1), :], coef_ref[pl.ds(row + 1, 1), :]
    fresh_odd = [one * e - o for e, o in zip(even, odd)]
    gains = [two * x for x in x2]
    fresh_even = [(g * one - 1.0) * e - g * o for g, e, o in zip(gains, even, odd)]
    return fresh_even, fresh_odd


def turn_lanes(chunk, per_block, q, seeds, even, odd):
    turned = q == lax.div(chunk, per_block) - 1
    if per_block > 1:
        turned = jnp.logical_and(turned, lax.rem(chunk, per_block) == 0)
    return [jnp.where(turned, s, e) for s, e in zip(seeds, even)], [jnp.where(turned, 0.0, o) for o in odd]


def recurrence_kernel(
    n_dev,
    vregs,
    pixel_total,
    rise_hbm,
    low_hbm,
    high_hbm,
    x_hbm,
    rows_hbm,
    u_hbm,
    rise_ref,
    low_ref,
    high_ref,
    x_ref,
    rows_ref,
    u_ref,
    even_ref,
    sems,
):
    pairs = LMAX // (2 * n_dev)
    per_block = n_dev // CHUNK
    chunks = step_blocks(n_dev) * per_block
    total = chunks * CHUNK
    piece = STREAMED // PIECES
    ends = [0, 2 * piece * CHUNK, STREAMED * CHUNK, total]
    parts = [(x_hbm, x_ref)]
    for start, stop in zip(ends, ends[1:]):
        for src, dst in ((rise_hbm, rise_ref), (low_hbm, low_ref), (high_hbm, high_ref)):
            reach = 0 if src is rise_hbm else 2 * n_dev
            first = start + reach if start else 0
            span = pl.ds(first, stop + reach - first)
            parts.append((src.at[span], dst.at[span]))
    copies = fetch(parts, sems)
    d = device_index()
    lane = lax.broadcasted_iota(jnp.int32, (8, LANES), 1)
    sub = lax.broadcasted_iota(jnp.int32, (8, LANES), 0)
    q = lax.rem(lane, pairs)
    m_low = (d + n_dev * q).astype(F32)
    m_high = (LMAX - 1.0) - m_low
    weight_low = jnp.where(m_low == 0.0, 1.0, 2.0) / pixel_total
    weight_high = jnp.full((8, LANES), 2.0 / pixel_total, F32)
    l_low = sub.astype(F32) + (d.astype(F32) - n_dev)
    l_high = sub.astype(F32) + m_high
    for copy in copies[:4]:
        copy.wait()
    x2 = [x_ref[1, 8 * v : 8 * v + 8, :] for v in range(vregs)]
    logs = [x_ref[2, 8 * v : 8 * v + 8, :] for v in range(vregs)]
    seed_low = [jnp.exp(m_low * g) for g in logs]
    seed_high = [jnp.exp(m_high * g) for g in logs]

    def coefficients(start, stop):
        many = max(n for n in range(1, 13) if (stop - start) % n == 0)

        def some(group, carry):
            fresh = []
            for step in range(many):
                chunk = start + group * many + step
                is_low = q < lax.div(chunk, per_block)
                weight = jnp.where(is_low, weight_low, weight_high)
                first = jnp.where(is_low, l_low, l_high) + (chunk * CHUNK).astype(F32)
                for i in range(CHUNK // 8):
                    tau = pl.multiple_of(chunk * CHUNK, CHUNK) + 8 * i
                    low = low_ref[pl.ds(tau + 2 * d, 8), :]
                    high = high_ref[pl.ds(tau + 2 * (n_dev - 1 - d), 8), :]
                    product = rise_ref[pl.ds(tau, 8), :] * jnp.where(is_low, low, high)
                    degree = first + 8.0 * i
                    coef = product * (degree * math.pi + 0.5 * math.pi)
                    fresh.append((tau, coef, jnp.where(degree < LMAX, product * weight, 0.0)))
            for tau, coef, weight in fresh:
                rows_ref[pl.ds(tau, 8), :] = coef
                rows_ref[pl.ds(total + tau, 8), :] = weight
            return carry

        lax.fori_loop(0, (stop - start) // many, some, 0)

    def steps(chunk, state):
        even, odd = turn_lanes(chunk, per_block, q, seed_low, list(state[:vregs]), list(state[vregs:]))
        first = pl.multiple_of(chunk * CHUNK, CHUNK)
        start = pl.multiple_of(chunk * (CHUNK * 4 * vregs), CHUNK * 4 * vregs)
        for s in range(0, CHUNK, 2):
            fresh_even, fresh_odd = advance(rows_ref, first + s, even, odd, x2)
            for v in range(vregs):
                u_ref[pl.ds(start + 8 * (s // 2 * vregs + v), 8), :] = even[v]
            even, odd = fresh_even, fresh_odd
        return (*even, *odd)

    zero = jnp.zeros((8, LANES), F32)
    state = (*seed_high, *([zero] * vregs))
    size = piece * CHUNK * 4 * vregs
    out = []

    def send(src, dst, sem):
        out.append(pltpu.make_async_copy(src, dst, sems.at[sem]))
        out[-1].start()

    for p in range(PIECES):
        first = p * piece
        if p == 0:
            coefficients(0, 2 * piece)
        if p == 2:
            for copy in copies[4:7]:
                copy.wait()
            coefficients(2 * piece, STREAMED)
        state = lax.fori_loop(first // 2, (first + piece) // 2, lambda h, s: steps(2 * h + 1, steps(2 * h, s)), state)
        extra = 0
        if p == PIECES - 1:
            extra = 16 * vregs
            for v in range(2 * vregs):
                u_ref[PIECES * size + 8 * v : PIECES * size + 8 * v + 8, :] = state[v]
        span = pl.ds(p * size, size + extra)
        send(u_ref.at[span], u_hbm.at[span], 10 + p)
    cut = STREAMED * CHUNK
    for i in range(cut // 16):
        even_ref[8 * i : 8 * i + 8, :] = rows_ref[pl.ds(16 * i, 8, stride=2), :]
    send(even_ref, rows_hbm.at[pl.ds(0, cut // 2)], 10 + PIECES)
    for copy in copies[7:]:
        copy.wait()
    coefficients(STREAMED, chunks)
    rest = 2 * total - cut
    send(rows_ref.at[pl.ds(cut, rest)], rows_hbm.at[pl.ds(cut // 2, rest)], 11 + PIECES)
    for copy in out:
        copy.wait()


def legendre_rows(n_dev, lats):
    pairs = LMAX // (2 * n_dev)
    vregs = lats * pairs // (8 * LANES)
    total = step_blocks(n_dev) * n_dev
    cut = STREAMED * CHUNK
    tables = [jnp.asarray(t) for t in recurrence_tables(n_dev, lats)]
    rows = jax.ShapeDtypeStruct((2 * total, LANES), F32)
    u = jax.ShapeDtypeStruct((cut * 4 * vregs + 16 * vregs, LANES), F32)
    return pl.pallas_call(
        functools.partial(recurrence_kernel, n_dev, vregs, float(2 * lats * CYCLE_PIX)),
        out_shape=(jax.ShapeDtypeStruct((2 * total - cut // 2, LANES), F32), u),
        in_specs=[ANY] * 4,
        out_specs=(ANY, ANY),
        scratch_shapes=[pltpu.VMEM(t.shape, t.dtype) for t in [*tables, rows, u]]
        + [pltpu.VMEM((cut // 2, LANES), F32), pltpu.SemaphoreType.DMA((12 + PIECES,))],
        compiler_params=pltpu.CompilerParams(vmem_limit_bytes=VMEM_LIMIT),
        cost_estimate=pl.CostEstimate(flops=total * 8 * LANES * vregs * 8, bytes_accessed=25000000, transcendentals=0),
        name="legendre_rows",
    )(*tables)


def power_tables(n_dev, n_blk, lats, slots):
    pairs = LMAX // (2 * n_dev)
    cycles_all = 2 * lats
    n_mblk = n_dev // n_blk
    cycle_dev = slots // SEGS
    r_band = cycle_dev * n_mblk
    col = 2 * n_blk * cycle_dev
    pick = np.zeros((4 * lats + 16, n_dev * col))

    def put(row, cycle, phase, weight):
        band, inner = divmod(cycle, r_band)
        j, k = divmod(inner, cycle_dev)
        for s in range(n_blk):
            pick[row, (s * n_mblk + j) * col + (band * cycle_dev + k) * 2 + phase] += weight

    for phase in range(2):
        for n in range(lats):
            for odd in range(2):
                row = (2 * phase + odd) * lats + n
                put(row, n, phase, 1.0)
                if n:
                    put(row, cycles_all - n, phase, -1.0 if odd else 1.0)
        put(4 * lats + phase, lats, phase, 1.0)

    lane = np.arange(LANES)
    band_of = (3 * pairs - 2 - lane) % LANES
    copies = LANES // n_dev
    spread = (band_of[None, :] % copies == (lane // n_dev)[:, None]) & (band_of[None, :] < 2 * pairs)
    gather = band_of[None, :] // copies == np.arange(LMAX // LANES)[:, None]
    return (
        pick.astype(jnp.bfloat16),
        recurrence_tables(n_dev, lats)[3],
        spread.astype(np.float32),
        gather.astype(jnp.bfloat16),
    )


def exact_dot(zero_one, x, dims):
    total = None
    for _ in range(3):
        part = x.astype(BF16)
        x = x - part.astype(F32)
        term = lax.dot_general(zero_one, part, (dims, ((), ())), preferred_element_type=F32)
        total = term if total is None else total + term
    return total


def power_kernel(
    n_dev,
    vregs,
    rows_hbm,
    u_hbm,
    got_ref,
    pick_ref,
    x_ref,
    spread_ref,
    gather_ref,
    out_ref,
    rows_ref,
    u_ref,
    f_ref,
    prod_a,
    prod_b,
    sum_ref,
    accl_ref,
    acch_ref,
    sems,
):
    pairs = LMAX // (2 * n_dev)
    all_steps = step_blocks(n_dev) * n_dev
    cut = STREAMED * CHUNK
    size = cut // PIECES * 4 * vregs
    spans = [pl.ds(p * size, size) for p in range(PIECES)]
    states, soon = pl.ds(PIECES * size, 16 * vregs), pl.ds(cut // 2, 8 * CHUNK)
    later = pl.ds(cut // 2 + 8 * CHUNK, all_steps - cut - 8 * CHUNK)
    early, weights = pl.ds(0, cut // 2), pl.ds(all_steps - cut // 2, all_steps)
    copies = fetch(
        [
            (u_hbm.at[states], u_ref.at[states]),
            (rows_hbm.at[soon], rows_ref.at[soon]),
        ],
        sems,
    )
    d = device_index()
    reps = LANES // pairs
    lats = vregs * 8 * reps
    per_block = n_dev // CHUNK
    blocks = step_blocks(n_dev)
    chunks = blocks * per_block
    lane = lax.broadcasted_iota(jnp.int32, (8, LANES), 1)
    sub = lax.broadcasted_iota(jnp.int32, (8, LANES), 0)
    q = lax.rem(lane, pairs)
    head = lane < pairs
    sign = jnp.where(sub % 4 == 0, 1.0, jnp.where(sub % 4 == 2, -1.0, 0.0)).astype(F32)
    accl_ref[...] = jnp.zeros_like(accl_ref)
    acch_ref[...] = jnp.zeros_like(acch_ref)
    prod_b[...] = jnp.zeros_like(prod_b)

    f_all = exact_dot(pick_ref[...], got_ref[...], ((1,), (0,)))

    def store(slot, value):
        f_ref[8 * slot : 8 * slot + 8, :] = value

    def load(slot):
        return f_ref[8 * slot : 8 * slot + 8, :]

    for phase in range(2):
        for odd in range(2):
            for v in range(vregs):
                for part in range(2):
                    pieces = []
                    for h in range(reps):
                        row = (2 * phase + odd) * lats + (v * reps + h) * 8
                        pieces.append(f_all[row : row + 8, part * pairs : (part + 1) * pairs])
                    value = jnp.concatenate(pieces, axis=1)
                    if odd:
                        value = value * x_ref[0, 8 * v : 8 * v + 8, :]
                    store(((phase * 2 + odd) * vregs + v) * 2 + part, value)
    base = 8 * vregs
    for phase in range(2):
        row = f_all[4 * lats + phase : 4 * lats + phase + 1, :]
        if 2 * pairs < LANES:
            row = jnp.concatenate([row, jnp.zeros((1, LANES - 2 * pairs), F32)], axis=1)
        store(base + phase, jnp.broadcast_to(row, (8, LANES)) * sign)

    def spectra_now(chunk):
        is_low = q < lax.div(chunk, per_block)

        def now(o, v, p):
            return jnp.where(is_low, load((o * vregs + v) * 2 + p), load(((2 + o) * vregs + v) * 2 + p))

        return [[[now(o, v, p) for p in range(2)] for v in range(vregs)] for o in range(2)]

    def product(s, u, now, prod_ref):
        for part in range(2):
            value = u[0] * now[s % 2][0][part]
            for v in range(1, vregs):
                value = value + u[v] * now[s % 2][v][part]
            prod_ref[part, pl.ds((s // 8) * 8 * PITCH + s % 8, 8, stride=PITCH), :] = value

    def products(chunk, prod_ref, odd):
        now = spectra_now(chunk)
        start = pl.multiple_of(chunk * (CHUNK * 4 * vregs), CHUNK * 4 * vregs)
        first = pl.multiple_of(chunk * (CHUNK // 2), CHUNK // 2)
        _, odd = turn_lanes(chunk, per_block, q, seed_low, odd, odd)
        for s in range(0, CHUNK, 2):
            even = [u_ref[pl.ds(start + 8 * (s // 2 * vregs + v), 8), :] for v in range(vregs)]
            one = rows_ref[pl.ds(first + s // 2, 1), :]
            odd = [one * e - o for e, o in zip(even, odd)]
            product(s, even, now, prod_ref)
            product(s + 1, odd, now, prod_ref)
        return odd

    def steps(chunk, prod_ref, state):
        now = spectra_now(chunk)
        even, odd = turn_lanes(chunk, per_block, q, seed_low, list(state[:vregs]), list(state[vregs:]))
        first = pl.multiple_of(chunk * CHUNK - cut // 2, CHUNK // 2)
        for s in range(0, CHUNK, 2):
            fresh_even, fresh_odd = advance(rows_ref, first + s, even, odd, x2)
            product(s, even, now, prod_ref)
            product(s + 1, fresh_odd, now, prod_ref)
            even, odd = fresh_even, fresh_odd
        return (*even, *odd)

    def reduce(chunk, prod_ref):
        for i in range(CHUNK // 8):
            for part in range(2):
                rows = [prod_ref[part, pl.ds((8 * i + s) * PITCH, 8), :] for s in range(8)]
                while len(rows) > 1:
                    rows = [a + b for a, b in zip(rows[::2], rows[1::2])]
                sum_ref[part, pl.ds(pl.multiple_of(chunk * CHUNK, CHUNK) + 8 * i, 8), :] = rows[0]

    def two_inline(h, state):
        state = steps(2 * h, prod_a, state)
        reduce(jnp.maximum(2 * h - 1, STREAMED), prod_b)
        state = steps(2 * h + 1, prod_b, state)
        reduce(2 * h, prod_a)
        return state

    def two_streamed(h, odd):
        odd = products(2 * h, prod_a, list(odd))
        reduce(jnp.maximum(2 * h - 1, 0), prod_b)
        odd = products(2 * h + 1, prod_b, odd)
        reduce(2 * h, prod_a)
        return tuple(odd)

    m_low = (d + n_dev * q).astype(F32)
    x2 = [x_ref[1, 8 * v : 8 * v + 8, :] for v in range(vregs)]
    seed_low = [jnp.exp(m_low * x_ref[2, 8 * v : 8 * v + 8, :]) for v in range(vregs)]
    for copy in copies:
        copy.wait()
    moved = [(rows_hbm.at[span], rows_ref.at[span]) for span in (later, early)] + [(u_hbm.at[span], u_ref.at[span]) for span in spans]
    moved.append((rows_hbm.at[weights], rows_ref.at[weights]))
    copies = [pltpu.make_async_copy(src, dst, sems.at[2 + i]) for i, (src, dst) in enumerate(moved)]
    for copy in copies:
        copy.start()
    state = [u_ref[PIECES * size + 8 * v : PIECES * size + 8 * v + 8, :] for v in range(2 * vregs)]
    state = lax.fori_loop(STREAMED // 2, STREAMED // 2 + 4, two_inline, tuple(state), unroll=True)
    copies[0].wait()
    lax.fori_loop(STREAMED // 2 + 4, chunks // 2, two_inline, tuple(state), unroll=True)
    reduce(chunks - 1, prod_b)
    piece = STREAMED // PIECES
    odd = (jnp.zeros((8, LANES), F32),) * vregs
    copies[1].wait()
    for p in range(PIECES):
        copies[2 + p].wait()
        odd = lax.fori_loop(p * piece // 2, (p + 1) * piece // 2, two_streamed, odd)
    reduce(STREAMED - 1, prod_b)
    copies[-1].wait()

    def packed(tau):
        re, im = sum_ref[0, pl.ds(tau, 8), :], sum_ref[1, pl.ds(tau, 8), :]
        if 2 * pairs == LANES:
            return jnp.where(head, re, im) + pltpu.roll(jnp.where(head, im, re), pairs, 1)
        step = pairs
        while step < LANES:
            re, im = re + pltpu.roll(re, step, 1), im + pltpu.roll(im, step, 1)
            step *= 2
        return jnp.where(head, re, jnp.where(lane < 2 * pairs, im, 0.0))

    def powers(first, count, with_high):
        tiles = n_dev // 8
        places = [(i, j) for j in range(count) for i in range(tiles)]
        taus = [pl.multiple_of((first + j) * n_dev, n_dev) + 8 * i for i, j in places]
        lows = [q < first + j for j in range(count)]
        flats = [load(base)] * count
        if with_high:
            flats = [jnp.where(low, load(base), load(base + 1)) for low in lows]
        values = [packed(tau) for tau in taus]
        values = [v + flats[j] for v, (_, j) in zip(values, places)]
        values = [v * v * rows_ref[pl.ds(all_steps - cut // 2 + tau, 8), :] for v, tau in zip(values, taus)]
        low_parts = values
        if with_high:
            low_parts = [jnp.where(lows[j], v, 0.0) for v, (_, j) in zip(values, places)]
            high_parts = [v - low for v, low in zip(values, low_parts)]
        sums = [jnp.sum(v, axis=1, keepdims=True) for v in low_parts]
        if with_high:
            shifts = [count - 1 - j for _, j in places]
            high_parts = [pltpu.roll(v, shift, 1) if shift else v for v, shift in zip(high_parts, shifts)]
        for i in range(tiles):
            total = accl_ref[8 * i : 8 * i + 8, :]
            for j in range(count):
                target = lax.rem(3 * pairs - 1 - (first + j) + 2 * LANES, LANES)
                total = total + jnp.where(lane == target, sums[j * tiles + i], 0.0)
            accl_ref[8 * i : 8 * i + 8, :] = total
            if with_high:
                total = pltpu.roll(acch_ref[8 * i : 8 * i + 8, :], count, 1)
                for j in range(count):
                    total = total + high_parts[j * tiles + i]
                acch_ref[8 * i : 8 * i + 8, :] = total

    many = 1024 // n_dev
    half = pairs // many

    def both_halves(g, carry):
        powers(g * many, many, True)
        return carry

    def low_half(g, carry):
        powers(g * many, many, False)
        return carry

    lax.fori_loop(0, half, both_halves, 0)
    lax.fori_loop(half, blocks // many, low_half, 0)
    if blocks % many:
        powers(jnp.int32(blocks - blocks % many), blocks % many, False)

    rows = lax.broadcasted_iota(jnp.int32, (n_dev, LANES), 0)

    def shifted(acc, shift):
        rolled = pltpu.roll(acc, shift, 0)
        return jnp.where(rows < shift, pltpu.roll(rolled, LANES - 1, 1), rolled)

    lanes = lax.broadcasted_iota(jnp.int32, (n_dev, LANES), 1)
    high = acch_ref[...] + pltpu.roll(acch_ref[...], LANES - pairs, 1)
    high = jnp.where(jnp.logical_and(lanes >= pairs - 1, lanes < 2 * pairs - 1), high, 0.0)
    power = shifted(accl_ref[...], d) + shifted(high, n_dev - 1 - d)
    tall = jnp.concatenate([power] * (LANES // n_dev), axis=0) * spread_ref[...]
    out_ref[...] = exact_dot(gather_ref[...], tall, ((1,), (1,)))


def power_of_orders(rows, u, got, n_dev, n_blk, lats, slots):
    pairs = LMAX // (2 * n_dev)
    vregs = lats * pairs // (8 * LANES)
    tables = [jnp.asarray(t) for t in power_tables(n_dev, n_blk, lats, slots)]
    prod = pltpu.VMEM((2, CHUNK * PITCH, LANES), F32)
    return pl.pallas_call(
        functools.partial(power_kernel, n_dev, vregs),
        out_shape=jax.ShapeDtypeStruct((LMAX // LANES, LANES), F32),
        in_specs=[ANY] * 2 + [VMEM] * 5,
        out_specs=VMEM,
        scratch_shapes=[pltpu.VMEM(t.shape, t.dtype) for t in [rows, u]]
        + [
            pltpu.VMEM((8 * (8 * vregs + 2), LANES), F32),
            prod,
            prod,
            pltpu.VMEM((2, step_blocks(n_dev) * n_dev, LANES), F32),
            pltpu.VMEM((n_dev, LANES), F32),
            pltpu.VMEM((n_dev, LANES), F32),
            pltpu.SemaphoreType.DMA((5 + PIECES,)),
        ],
        compiler_params=pltpu.CompilerParams(vmem_limit_bytes=POWER_VMEM),
        cost_estimate=pl.CostEstimate(flops=u.size * 4, bytes_accessed=1000000, transcendentals=0),
        name="order_power",
    )(rows, u, got, *tables)


def tree_sum(parts):
    while len(parts) > 1:
        parts = [a + b for a, b in zip(parts[::2], parts[1::2])]
    return parts[0]


def exchange(value, bits, n_dev):
    parts = [value]
    for chosen in range(1, 1 << len(bits)):
        flip = sum(bit for i, bit in enumerate(bits) if chosen >> i & 1)
        parts.append(lax.ppermute(value, ("blk", "mblk"), [(i, i ^ flip) for i in range(n_dev)]))
    return parts


def finish_kernel(*refs):
    *part_refs, model_ref, cl_ref, misfit_ref = refs
    cl = tree_sum([ref[...] for ref in part_refs])
    model = model_ref[...]
    cl_ref[...] = cl
    error = (cl - model) / model
    squares = jnp.sum(error * error, axis=0, keepdims=True)
    misfit_ref[...] = jnp.sum(squares, axis=1, keepdims=True) * (1.0 / LMAX)


def finish(parts, model_cl):
    shape = parts[0].shape
    cl, misfit = pl.pallas_call(
        finish_kernel,
        out_shape=(jax.ShapeDtypeStruct(shape, F32), jax.ShapeDtypeStruct((1, 1), F32)),
        in_specs=[VMEM] * (len(parts) + 1),
        out_specs=(VMEM, VMEM),
        compiler_params=pltpu.CompilerParams(vmem_limit_bytes=2 * 1024 * 1024),
        name="finish",
    )(*parts, model_cl.reshape(shape))
    return cl.reshape(LMAX), misfit.reshape(())


def on_device(pixels, block_ids, block_mask, model_cl):
    n_blk = lax.axis_size("blk")
    n_mblk = lax.axis_size("mblk")
    n_dev = n_blk * n_mblk
    slots = pixels.shape[0]
    cycles = n_blk * slots // SEGS
    lats = slots * n_dev // SEGS // 2
    pairs = LMAX // (2 * n_dev)

    rows, u = legendre_rows(n_dev, lats)
    sent = cycle_spectra(pixels, block_ids, block_mask, n_dev, n_blk)
    got = lax.all_to_all(sent.reshape(n_dev, 2 * cycles, 2 * pairs), ("blk", "mblk"), 0, 0, tiled=True)
    got = got.reshape(n_dev * 2 * cycles, 2 * pairs)
    power = power_of_orders(rows, u, got, n_dev, n_blk, lats, slots)

    inner = [1 << i for i in range(n_mblk.bit_length() - 1)]
    outer = [n_mblk << i for i in range(n_blk.bit_length() - 1)]
    rounds = [inner[-1:], inner[-2:-1] + outer]
    inner = inner[:-2]
    while inner:
        rounds.append(inner[-2:])
        inner = inner[:-2]
    parts = [power]
    for bits in rounds:
        parts = exchange(tree_sum(parts), bits, n_dev)
    return finish(parts, model_cl)


def solution(mesh):
    in_specs = (P(("blk", "mblk"), None), P(("blk", "mblk")), P(("blk", "mblk")), P())
    out_specs = (P(), P())
    return jax.shard_map(
        on_device, mesh=mesh, in_specs=in_specs, out_specs=out_specs, check_vma=False
    )
```
